32 devices in a mesh: seq: 8 (over z, y), mp: 4 (over x, core).
Axes of the slice: x: 2, y: 2, z: 4, core: 2. Of those that a mesh axis runs over, the one named last changes fastest.
Arguments:
- tokens: bfloat16 [4608, 2048], P('seq'), may hold values from -6 to 6
- attn_gain: bfloat16 [2048], replicated, may hold values from 0.5 to 1.5
- w_input: bfloat16 [2048, 2048], P(None, 'mp'), may hold values from -0.125 to 0.125
- w_forget: bfloat16 [2048, 2048], P(None, 'mp'), may hold values from -0.125 to 0.125
- w_rgate: bfloat16 [2048, 2048], P(None, 'mp'), may hold values from -0.125 to 0.125
- gnorm_gain: bfloat16 [2048], P('mp'), may hold values from 0.5 to 1.5
- lower_bound: float32 [2048], P('mp'), may hold values from 0.4 to 0.99999
- w_out: bfloat16 [2048, 2048], P('mp'), may hold values from -0.125 to 0.125
- mlp_gain: bfloat16 [2048], replicated, may hold values from 0.5 to 1.5
- w_gate: bfloat16 [2048, 5632], P(None, 'mp'), may hold values from -0.125 to 0.125
- w_up: bfloat16 [2048, 5632], P(None, 'mp'), may hold values from -0.125 to 0.125
- w_down: bfloat16 [5632, 2048], P('mp'), may hold values from -0.078125 to 0.078125
- local_lengths: int32 [8, 3], P('seq'), may hold values from 1 to 240, 320 in all within a row
- cotangent: bfloat16 [4608, 2048], P('seq'), may hold values from -6 to 6
Outputs:
- mixed_out: bfloat16 [4608, 2048], P('seq')
- grad_tokens: bfloat16 [4608, 2048], P('seq')
- grad_attn_gain: float32 [2048], P('seq')
- grad_w_input: float32 [2048, 2048], P('seq', 'mp')
- grad_w_forget: float32 [2048, 2048], P('seq', 'mp')
- grad_w_rgate: float32 [2048, 2048], P('seq', 'mp')
- grad_gnorm_gain: float32 [4, 512], P('mp', 'seq')
- grad_lower_bound: float32 [4, 512], P('mp', 'seq')
- grad_w_out: float32 [2048, 2048], P('mp', 'seq')
- grad_mlp_gain: float32 [2048], P('seq')
- grad_w_gate: float32 [2048, 5632], P('seq', 'mp')
- grad_w_up: float32 [2048, 5632], P('seq', 'mp')
- grad_w_down: float32 [5632, 2048], P('mp', 'seq')
The draws below stay inside these ranges and needn't reach their ends.
Inputs may be any that keep to these rules, and one draw needn't show every extreme that they name: `local_lengths`: each row holds the lengths of the 3 short sequences of one block, in order; they sum to 320, the longest is 240.
All inputs are finite; a program needn't handle non-finite values.
Results may differ from the reference program's by a relative error of at most 0.008.
Values sent between devices are 32-bit elements; how exact they have to be, the bound alone decides.
No kernel may reach another device: no remote copies, remote signals or barrier semaphores. Data moves between devices by JAX's collectives and lax.ppermute only.
A program may use at most 256 MiB of HBM per device.

```python
import math
import jax
import jax.numpy as jnp
import numpy as np
from jax import lax

D = 2048
FF = 5632
LCHUNK = 256
LOCAL = 320
DOCS = 3
SHORT_MOST = 240
TOK_DEV = 576
CYCLE = 8
TOKENS = 4608
CH_MP = 512
N_MP = 4


def draw_lower_bound(key, part):
    key = jax.random.fold_in(key, 11)
    uniform_draw = jax.random.uniform(key, (D,), jnp.float32)
    least_rate = 1e-05
    most_rate = 0.6
    forget_rate = jnp.exp(jnp.log(least_rate) + uniform_draw * (jnp.log(most_rate) - jnp.log(least_rate)))
    return 1.0 - forget_rate


def levels(rng, extent, split, low, high):
    def one(dim, blocks):
        draws = jax.random.uniform(jax.random.fold_in(jax.random.fold_in(rng, 6), dim), (blocks,), jnp.float32, low / len(split), high / len(split))
        return jnp.repeat(jnp.exp(draws), extent[dim] // blocks).reshape((-1,) + (1,) * (len(extent) - dim - 1))

    loudness = one(*split[0])
    for cut in split[1:]:
        loudness = loudness * one(*cut)
    return loudness


def length_profile(count, total, most, skew):
    loads = [(1 << 20) // math.isqrt(rank ** skew) + 1 for rank in range(2, count + 1)]
    surplus, holding = total - most - (count - 1), [1] * (count - 1)
    while surplus > 0:
        candidates = [i for i in range(count - 1) if holding[i] < most]
        whole, left = sum([loads[i] for i in candidates]), surplus
        for i in candidates:
            more = min(most - holding[i], max(1, left * loads[i] // whole), surplus)
            holding[i] = holding[i] + more
            surplus = surplus - more
    return np.array([most] + holding)


def uneven_parts(stream_key, amount, total, reach, skew):
    if amount == 2:
        one = jax.random.randint(stream_key, (), max(1, total - reach), min(reach, total - 1) + 1)
        return jnp.stack([one, total - one])
    sizes = jnp.asarray(length_profile(amount, total, reach, skew), jnp.int32)
    twos = (amount - 1) // 2
    giver, sink = sizes[1:1 + 2 * twos:2], sizes[2:2 + 2 * twos:2]
    margin = jnp.minimum(giver - 1, reach - sink)
    shifted = jax.random.randint(jax.random.fold_in(stream_key, 1), (twos,), 0, 1 << 20) % (margin + 1)
    sizes = sizes.at[1:1 + 2 * twos:2].set(giver - shifted).at[2:2 + 2 * twos:2].set(sink + shifted)
    return sizes[jax.random.permutation(jax.random.fold_in(stream_key, 2), amount)]


def bell_draw(key, dims, scale, most, cuts=(), kind=jnp.bfloat16):
    loudness = levels(key, dims, cuts, -0.22, 0.18) if cuts else 1.0
    values = jax.random.normal(key, dims, jnp.float32) * scale * loudness
    return jnp.minimum(jnp.maximum(values, -most), most).astype(kind)


def setup_inputs(seed: int = 0) -> dict:
    key_list = jax.random.split(jax.random.key(seed), 15)
    tokens = bell_draw(key_list[0], (TOKENS, D), 1.0, 6.0, ((0, 8),))
    attn_gain = jnp.clip(1.0 + 0.1 * jax.random.normal(key_list[1], (D,), jnp.float32), 0.5, 1.5).astype(jnp.bfloat16)
    w_input = bell_draw(key_list[2], (D, D), D ** -0.5, 0.125, ((1, 4),))
    w_forget = bell_draw(key_list[3], (D, D), D ** -0.5, 0.125, ((1, 4),))
    w_rgate = bell_draw(key_list[4], (D, D), D ** -0.5, 0.125, ((1, 4),))
    gnorm_gain = jnp.clip(1.0 + 0.1 * jax.random.normal(key_list[5], (D,), jnp.float32), 0.5, 1.5).astype(jnp.bfloat16)
    lower_bound = draw_lower_bound(jax.random.fold_in(key_list[14], 71), 0)
    w_out = bell_draw(key_list[7], (D, D), D ** -0.5, 0.125, ((0, 4),))
    mlp_gain = jnp.clip(1.0 + 0.1 * jax.random.normal(key_list[8], (D,), jnp.float32), 0.5, 1.5).astype(jnp.bfloat16)
    w_gate = bell_draw(key_list[9], (D, FF), D ** -0.5, 0.125, ((1, 4),))
    w_up = bell_draw(key_list[10], (D, FF), D ** -0.5, 0.125, ((1, 4),))
    w_down = bell_draw(key_list[11], (FF, D), FF ** -0.5, 0.078125, ((0, 4),))
    local_lengths = jax.vmap(lambda own: uneven_parts(own, DOCS, LOCAL, SHORT_MOST, 2))(jax.random.split(key_list[12], CYCLE)).reshape((CYCLE, DOCS)).astype(jnp.int32)
    cotangent = bell_draw(key_list[13], (TOKENS, D), 1.0, 6.0, ((0, 8),))
    return {"tokens": tokens, "attn_gain": attn_gain, "w_input": w_input, "w_forget": w_forget, "w_rgate": w_rgate, "gnorm_gain": gnorm_gain, "lower_bound": lower_bound, "w_out": w_out, "mlp_gain": mlp_gain, "w_gate": w_gate, "w_up": w_up, "w_down": w_down, "local_lengths": local_lengths, "cotangent": cotangent}


norm_eps = 1e-06

@jax.custom_vjp
def low(v):
    return lax.optimization_barrier(v.astype(jnp.bfloat16)).astype(jnp.float32)

@jax.custom_vjp
def low_back(v):
    return v

def low_keep(v):
    return (low(v), None)

def low_pass(kept, grad):
    return (grad,)

def back_keep(v):
    return (v, None)

def back_low(kept, grad):
    return (low(grad),)
low.defvjp(low_keep, low_pass)
low_back.defvjp(back_keep, back_low)

def hidot(left, right):
    return jnp.dot(left, right, precision=lax.Precision.HIGHEST, preferred_element_type=jnp.float32)

def rms_hat(values):
    return values * lax.rsqrt(lax.optimization_barrier(jnp.mean(values * values, axis=-1, keepdims=True)) + norm_eps)

def compose(earlier, later):
    return (earlier[0] * later[0], later[0] * earlier[1] + later[1])

def linear_scan(decay, source, along):
    return lax.associative_scan(compose, (decay, source), axis=along)

def local_starts(local_lengths):
    offsets = (jnp.cumsum(local_lengths, axis=1) - local_lengths).astype(jnp.int32)
    places = jnp.arange(LOCAL, dtype=jnp.int32)
    return jnp.any(places[None, :, None] == offsets[:, None, :], axis=2)

def recurrence(forget, drive, starts):
    forget_rows = forget.reshape(CYCLE, TOK_DEV, D)
    drive_rows = drive.reshape(CYCLE, TOK_DEV, D)
    long_forget = forget_rows[:, :LCHUNK].reshape(CYCLE * LCHUNK, D)
    long_drive = drive_rows[:, :LCHUNK].reshape(CYCLE * LCHUNK, D)
    long_decay, long_state = linear_scan(long_forget, long_drive, 0)
    short_part = forget_rows[:, LCHUNK:]
    short_forget = jnp.where(starts[:, :, None], jnp.zeros_like(short_part), short_part)
    short_decay, short_state = linear_scan(short_forget, drive_rows[:, LCHUNK:], 1)
    states = jnp.concatenate([long_state.reshape(CYCLE, LCHUNK, D), short_state], axis=1)
    return states.reshape(TOKENS, D)

def reference(tokens, attn_gain, w_input, w_forget, w_rgate, gnorm_gain, lower_bound, w_out, mlp_gain, w_gate, w_up, w_down, local_lengths, cotangent):
    starts = local_starts(local_lengths)

    def forward(stream, first_gain, proj_input, proj_forget, proj_rgate, state_gain, bound, proj_out, second_gain, proj_gate, proj_up, proj_down):
        normed_one = low(rms_hat(stream) * first_gain)
        pre_input = low_back(hidot(normed_one, proj_input))
        pre_forget = low_back(hidot(normed_one, proj_forget))
        pre_rgate = low_back(hidot(normed_one, proj_rgate))
        forget = bound + (1.0 - bound) * jax.nn.sigmoid(pre_forget)
        drive = jax.nn.silu(pre_input) * (1.0 - forget)
        states = recurrence(forget, drive, starts)
        gated = low(rms_hat(states) * state_gain * jax.nn.silu(pre_rgate))
        middle = stream + low_back(hidot(gated, proj_out))
        normed_two = low(rms_hat(middle) * second_gain)
        gate = low_back(hidot(normed_two, proj_gate))
        up_values = low_back(hidot(normed_two, proj_up))
        hidden = low(jax.nn.silu(gate) * up_values)
        return middle + low_back(hidot(hidden, proj_down))
    mixed, pullback = jax.vjp(forward, tokens.astype(jnp.float32), attn_gain.astype(jnp.float32), w_input.astype(jnp.float32), w_forget.astype(jnp.float32), w_rgate.astype(jnp.float32), gnorm_gain.astype(jnp.float32), lower_bound.astype(jnp.float32), w_out.astype(jnp.float32), mlp_gain.astype(jnp.float32), w_gate.astype(jnp.float32), w_up.astype(jnp.float32), w_down.astype(jnp.float32))
    grads = pullback(cotangent.astype(jnp.float32))
    return (mixed.astype(jnp.bfloat16), grads[0].astype(jnp.bfloat16), grads[1], grads[2], grads[3], grads[4], grads[5].reshape(N_MP, CH_MP), grads[6].reshape(N_MP, CH_MP), grads[7], grads[8], grads[9], grads[10], grads[11])
```

```python
import jax
import jax.numpy as jnp
from jax import lax
from jax.experimental import pallas as pl
from jax.experimental.pallas import tpu as pltpu
from jax.sharding import PartitionSpec as P

LCHUNK = 256
norm_eps = 1e-06
F32 = jnp.float32
BF16 = jnp.bfloat16

CORE_PAIRS = [(i, i ^ 1) for i in range(4)]
X_PAIRS = [(i, i ^ 2) for i in range(4)]
Y_PAIRS = [(i, i ^ 1) for i in range(8)]


def dot(left, right):
    return jnp.dot(left, right, preferred_element_type=F32)


def left_dot(left, right):
    return lax.dot_general(left, right, (((0,), (0,)), ((), ())), preferred_element_type=F32)


def right_dot(left, right):
    return lax.dot_general(left, right, (((1,), (1,)), ((), ())), preferred_element_type=F32)


def silu_slope(values):
    sig = jax.nn.sigmoid(values)
    return sig * (1.0 + values * (1.0 - sig))


def after(value, *others):
    return lax.optimization_barrier((value, *others))[0]


def round_kernel(flip_ref, first_ref, second_ref, out_ref):
    size = first_ref.shape[0]

    @pl.when(flip_ref[0] == 0)
    def _():
        out_ref[:size, :] = first_ref[...].astype(BF16)
        out_ref[size:, :] = second_ref[...].astype(BF16)

    @pl.when(flip_ref[0] != 0)
    def _():
        out_ref[:size, :] = second_ref[...].astype(BF16)
        out_ref[size:, :] = first_ref[...].astype(BF16)


def rounded(first, second, flip):
    size, width = first.shape
    block = 512
    spec = pl.BlockSpec((size, block), lambda i: (0, i))
    return pl.pallas_call(
        round_kernel,
        grid=(width // block,),
        in_specs=[pl.BlockSpec(memory_space=pltpu.SMEM), spec, spec],
        out_specs=pl.BlockSpec((2 * size, block), lambda i: (0, i)),
        out_shape=jax.ShapeDtypeStruct((2 * size, width), BF16),
        compiler_params=pltpu.CompilerParams(vmem_limit_bytes=16 * 1024 * 1024),
        cost_estimate=pl.CostEstimate(
            flops=size * width * 2, bytes_accessed=size * width * 12, transcendentals=0
        ),
        name="rounded",
    )(jnp.full((1,), flip, jnp.int32), first, second)


def scan_kernel(backward, a_ref, b_ref, x_ref, p_ref):
    rows, width = a_ref.shape
    place = lax.broadcasted_iota(jnp.int32, (8, width), 0)

    def group(start, carry_x, carry_p, with_product):
        a = a_ref[pl.ds(start, 8), :]
        b = b_ref[pl.ds(start, 8), :]
        for step in (1, 2, 4):
            shift = 8 - step if backward else step
            inside = place < 8 - step if backward else place >= step
            a_shift = jnp.where(inside, pltpu.roll(a, shift, 0), 1.0)
            b_shift = jnp.where(inside, pltpu.roll(b, shift, 0), 0.0)
            b = a * b_shift + b
            a = a * a_shift
        x = b + a * carry_x
        x_ref[pl.ds(start, 8), :] = x
        last = 0 if backward else 7
        carry_x = jnp.broadcast_to(x[last : last + 1, :], (8, width))
        if with_product:
            product = a * carry_p
            p_ref[pl.ds(start, 8), :] = product
            carry_p = jnp.broadcast_to(product[last : last + 1, :], (8, width))
        return carry_x, carry_p

    def run(first, count, with_product):
        def body(step, carry):
            place_of = count - 1 - step if backward else step
            start = pl.multiple_of(first + place_of * 8, 8)
            return group(start, *carry, with_product)

        lax.fori_loop(
            0,
            count,
            body,
            (jnp.zeros((8, width), F32), jnp.ones((8, width), F32)),
            unroll=4,
        )

    run(0, LCHUNK // 8, True)
    run(LCHUNK, (rows - LCHUNK) // 8, False)


def scan(a, b, backward):
    rows, width = a.shape
    block = 256
    spec = pl.BlockSpec((rows, block), lambda i: (0, i))
    return pl.pallas_call(
        lambda *refs: scan_kernel(backward, *refs),
        grid=(width // block,),
        in_specs=[spec, spec],
        out_specs=[spec, pl.BlockSpec((LCHUNK, block), lambda i: (0, i))],
        out_shape=[
            jax.ShapeDtypeStruct((rows, width), F32),
            jax.ShapeDtypeStruct((LCHUNK, width), F32),
        ],
        compiler_params=pltpu.CompilerParams(vmem_limit_bytes=16 * 1024 * 1024),
        cost_estimate=pl.CostEstimate(
            flops=rows * width * 12, bytes_accessed=rows * width * 14, transcendentals=0
        ),
        name="scan_back" if backward else "scan_forth",
    )(a, b)


def carry_of(decay, local, backward):
    count, mine = lax.axis_size("seq"), lax.axis_index("seq")
    ends = jnp.stack([decay, local])
    if count != 8:
        pieces = lax.all_gather(ends, "seq")
        order = jnp.arange(count)
        total = jnp.zeros_like(local)
        for step in range(count):
            i = count - 1 - step if backward else step
            use = (order[i] > mine) if backward else (order[i] < mine)
            total = jnp.where(use, pieces[i, 0] * total + pieces[i, 1], total)
        return total
    partner = lax.ppermute(ends, "seq", Y_PAIRS)
    first = (mine % 2 == 1) if backward else (mine % 2 == 0)
    early = jnp.where(first, ends, partner)
    late = jnp.where(first, partner, ends)
    pair = jnp.stack([early[0] * late[0], late[0] * early[1] + late[1]])
    total = jnp.zeros_like(local)
    got = []
    for hops in (3, 2, 1):
        if backward:
            pairs = [(i + 2 * hops, i) for i in range(8 - 2 * hops)]
        else:
            pairs = [(i, i + 2 * hops) for i in range(8 - 2 * hops)]
        got.append(lax.ppermute(pair, "seq", pairs))
    for piece in got:
        total = piece[0] * total + piece[1]
    return jnp.where(first, total, partner[0] * total + partner[1])


def small_psum(value):
    value = value + lax.ppermute(value, "mp", CORE_PAIRS)
    return value + lax.ppermute(value, "mp", X_PAIRS)


def summed_half(send, keep):
    value = keep + lax.ppermute(send, "mp", CORE_PAIRS)
    return value + lax.ppermute(value, "mp", X_PAIRS)


def butterfly(value, axis):
    count = lax.axis_size(axis)
    step = 1
    while step < count:
        value = value + lax.ppermute(value, axis, [(i, i ^ step) for i in range(count)])
        step *= 2
    return value


def chain(part):
    plane = lax.axis_index("seq") // 2
    parts = [part(jnp.bitwise_xor(slot, 3 - plane)) for slot in range(4)]

    def move(value, hops):
        pairs = [(2 * a + y, 2 * b + y) for a, b in hops for y in range(2)]
        return lax.ppermute(value, "seq", pairs)

    second = parts[1] + move(parts[0], [(0, 1), (3, 2)])
    up = move(second, [(0, 1), (1, 2)])
    down = move(second, [(3, 2), (2, 1)])
    up = jnp.where(plane == 1, parts[0], parts[2]) + up
    down = jnp.where(plane == 2, parts[0], parts[2]) + down
    up = move(up, [(0, 1), (1, 2), (2, 3)])
    down = move(down, [(3, 2), (2, 1), (1, 0)])
    return parts[3] + up + down


def per_device(
    tokens,
    attn_gain,
    w_input,
    w_forget,
    w_rgate,
    gnorm_gain,
    lower_bound,
    w_out,
    mlp_gain,
    w_gate,
    w_up,
    w_down,
    local_lengths,
    cotangent,
):
    rows, width = tokens.shape
    short_rows = rows - LCHUNK
    count, mine = lax.axis_size("seq"), lax.axis_index("seq")
    fast = count == 8
    core = lax.axis_index("mp") % 2
    side = mine % 2
    chunks = ((LCHUNK, short_rows), (0, LCHUNK))

    def half(value, own, chunk):
        first, size = chunk
        which = core if own else 1 - core
        return lax.dynamic_slice_in_dim(value, first + which * (size // 2), size // 2, 0)

    def swap_core(value):
        return lax.ppermute(value, "mp", CORE_PAIRS)

    def swap_y(value):
        return lax.ppermute(value, "seq", Y_PAIRS)

    def canonical(parts):
        out = []
        for own, other in (parts[1], parts[0]):
            out.append(jnp.where(core == 0, own, other))
            out.append(jnp.where(core == 0, other, own))
        return jnp.concatenate(out, axis=0)

    def side_columns(value, which):
        wide = value.reshape(value.shape[0], 4, 2, width // 8)
        return lax.dynamic_index_in_dim(wide, which, 2, keepdims=False).reshape(
            value.shape[0], width // 2
        )

    lengths_row = local_lengths[0]
    offsets = jnp.cumsum(lengths_row) - lengths_row
    starts = jnp.any(
        jnp.arange(short_rows, dtype=jnp.int32)[:, None] == offsets[None, :], axis=1
    )[:, None]

    cot_own = [(half(cotangent, True, c), half(cotangent, False, c)) for c in chunks]
    cot_rows = jnp.concatenate([part for pair in cot_own for part in pair], axis=0)
    d_hidden = right_dot(cot_rows, w_down)

    stream = tokens.astype(F32)
    first_gain = attn_gain.astype(F32)
    first_scale = lax.rsqrt(jnp.mean(stream * stream, axis=1, keepdims=True) + norm_eps)
    normed_one_wide = stream * first_scale * first_gain
    normed_one = normed_one_wide.astype(BF16)
    pre_forget = dot(normed_one, w_forget)
    pre_input = dot(normed_one, w_input)
    pre_rgate = dot(normed_one, w_rgate)
    forget_sig = jax.nn.sigmoid(pre_forget)
    forget = lower_bound + (1.0 - lower_bound) * forget_sig
    input_act = jax.nn.silu(pre_input)
    drive = input_act * (1.0 - forget)
    is_start = jnp.concatenate([jnp.zeros((LCHUNK, 1), bool), starts], axis=0)
    states_local, long_decay = scan(jnp.where(is_start, 0.0, forget), drive, False)
    carry_in = carry_of(long_decay[-1], states_local[LCHUNK - 1], False)

    state_gain = gnorm_gain.astype(F32)
    rgate_act = jax.nn.silu(pre_rgate)
    second_gain = mlp_gain.astype(F32)

    def row_scale(values):
        return lax.rsqrt(jnp.mean(values * values, axis=1, keepdims=True) + norm_eps)

    def glu(middle, d_hid):
        scale = row_scale(middle)
        hat = middle * scale
        normed = (hat * second_gain).astype(BF16)
        gate = dot(normed, w_gate)
        up = dot(normed, w_up)
        act = jax.nn.silu(gate)
        hidden = (act * up).astype(BF16)
        d_gate = (d_hid * up * silu_slope(gate)).astype(BF16)
        d_up = (d_hid * act).astype(BF16)
        return scale, hat, normed, hidden, d_gate, d_up

    states_of, scale_of, gated_of, middle_own, middle_other = [], [], [], [], []
    for index, (first, size) in enumerate(chunks):
        local = states_local[first : first + size]
        if index == 1:
            local = local + long_decay * carry_in[None, :]
        squares = small_psum(jnp.sum(local * local, axis=1))
        scale = lax.rsqrt(squares / width + norm_eps)[:, None]
        gated = local * scale * state_gain * rgate_act[first : first + size]
        gated16 = gated.astype(BF16)
        states_of.append(local)
        scale_of.append(scale)
        gated_of.append(gated)
        h = size // 2
        send = dot(lax.dynamic_slice_in_dim(gated16, (1 - core) * h, h, 0), w_out)
        keep = dot(lax.dynamic_slice_in_dim(gated16, core * h, h, 0), w_out)
        own = half(tokens, True, (first, size)).astype(F32) + summed_half(send, keep)
        middle_own.append(own)
        middle_other.append(swap_core(own))

    states = jnp.concatenate([states_of[1], states_of[0]], axis=0)
    state_scale = jnp.concatenate([scale_of[1], scale_of[0]], axis=0)
    gated_wide = jnp.concatenate([gated_of[1], gated_of[0]], axis=0)
    gated = gated_wide.astype(BF16)
    normed_state = states * state_scale

    offset = 0
    main, d_mid_own, d_mid_other, hat_grad, feeds = [], [], [], [], []
    for index, (first, size) in enumerate(chunks):
        h = size // 2
        middle = jnp.concatenate([middle_own[index], middle_other[index]], axis=0)
        scale, hat, normed, hidden, d_gate, d_up = glu(middle, d_hidden[offset : offset + size])
        offset += size
        main.append((normed, hidden, d_gate, d_up))
        send = right_dot(d_gate[h:], w_gate) + right_dot(d_up[h:], w_up)
        keep = right_dot(d_gate[:h], w_gate) + right_dot(d_up[:h], w_up)
        d_normed = summed_half(send, keep)
        hat, scale = hat[:h], scale[:h]
        hat_grad.append(jnp.sum(d_normed * hat, axis=0))
        e = d_normed * second_gain
        turn = scale * (e - hat * jnp.mean(e * hat, axis=1, keepdims=True))
        d_mid_own.append(cot_own[index][0].astype(F32) + turn)
        d_mid_other.append(cot_own[index][1].astype(F32) + swap_core(turn))
        hid = after(hidden, d_normed)
        feeds.append((dot(hid[h:], w_down), dot(hid[:h], w_down)))

    d_branch_wide = canonical(list(zip(d_mid_own, d_mid_other)))
    d_branch = d_branch_wide.astype(BF16)
    d_gated = right_dot(d_branch, w_out)
    grad_gnorm = jnp.sum(d_gated * normed_state * rgate_act, axis=0)
    d_rgate_wide = d_gated * normed_state * state_gain * silu_slope(pre_rgate)
    d_normed = d_gated * state_gain * rgate_act
    inner = small_psum(jnp.sum(d_normed * normed_state, axis=1))
    d_states = state_scale * (d_normed - normed_state * (inner / width)[:, None])
    shifted = jnp.concatenate([forget[1:], jnp.zeros_like(forget[:1])], axis=0)
    next_start = jnp.concatenate([is_start[1:], jnp.ones((1, 1), bool)], axis=0)
    links = jnp.where(next_start, 0.0, shifted)
    row = lax.broadcasted_iota(jnp.int32, (rows, 1), 0)
    links = jnp.where(row == LCHUNK - 1, 1.0, links)
    back_local, back_decay = scan(links, d_states, True)
    carried_in = carry_of(forget[0] * back_decay[0], forget[0] * back_local[0], True)
    carried = jnp.concatenate(
        [back_local[:LCHUNK] + back_decay * carried_in[None, :], back_local[LCHUNK:]], axis=0
    )
    states_prev = jnp.concatenate([carry_in[None, :], states[:-1]], axis=0)
    states_prev = jnp.where(is_start, 0.0, states_prev)
    d_forget = carried * (states_prev - input_act)
    d_input_wide = carried * (1.0 - forget) * silu_slope(pre_input)
    d_pforget_wide = d_forget * (1.0 - lower_bound) * forget_sig * (1.0 - forget_sig)
    grad_bound = jnp.sum(d_forget * (1.0 - forget_sig), axis=0)
    d_input = d_input_wide.astype(BF16)
    d_pforget = d_pforget_wide.astype(BF16)
    d_rgate = d_rgate_wide.astype(BF16)

    d_stream, first_grad = [], []
    for index, chunk in enumerate(chunks):
        both = []
        for own in (False, True):
            both.append(
                right_dot(half(d_input, own, chunk), w_input)
                + right_dot(half(d_pforget, own, chunk), w_forget)
                + right_dot(half(d_rgate, own, chunk), w_rgate)
            )
        d_normed_one = summed_half(*both)
        part = half(tokens, True, chunk).astype(F32)
        scale = row_scale(part)
        hat = part * scale
        first_grad.append(jnp.sum(d_normed_one * hat, axis=0))
        e = d_normed_one * first_gain
        turn = scale * (e - hat * jnp.mean(e * hat, axis=1, keepdims=True))
        d_stream.append((d_mid_own[index] + turn, d_mid_other[index] + swap_core(turn)))
    grad_tokens = canonical(d_stream).astype(BF16)

    mixed = []
    for own, other, feed in zip(middle_own, middle_other, feeds):
        value = summed_half(*feed)
        mixed.append((own + value, other + swap_core(value)))
    mixed_out = canonical(mixed).astype(BF16)

    pieces = jnp.concatenate([sum(first_grad), sum(hat_grad)])
    pieces = pieces + swap_core(pieces)
    vectors = butterfly(jnp.concatenate([pieces, grad_gnorm, grad_bound]), "seq")
    part = width // count
    grad_attn = lax.dynamic_slice_in_dim(vectors[:width], mine * part, part)
    grad_mlp = lax.dynamic_slice_in_dim(vectors[width : 2 * width], mine * part, part)
    channels = grad_gnorm.shape[0]
    small = channels // count
    grad_gnorm = lax.dynamic_slice_in_dim(
        vectors[2 * width : 2 * width + channels], mine * small, small
    )[None, :]
    grad_bound = lax.dynamic_slice_in_dim(vectors[2 * width + channels :], mine * small, small)[
        None, :
    ]

    normed_two, hidden, d_gate, d_up = (
        jnp.concatenate([main[0][i], main[1][i]], axis=0) for i in range(4)
    )

    if not fast:

        def scattered(value, dim):
            return lax.psum_scatter(value, "seq", scatter_dimension=dim, tiled=True)

        grads = (
            scattered(left_dot(normed_one, d_input), 0),
            scattered(left_dot(normed_one, d_pforget), 0),
            scattered(left_dot(normed_one, d_rgate), 0),
            scattered(left_dot(gated, d_branch), 1),
            scattered(left_dot(normed_two, d_gate), 0),
            scattered(left_dot(normed_two, d_up), 0),
            scattered(left_dot(hidden, cot_rows), 1),
        )
    else:
        cot_mine = jnp.concatenate([pair[0] for pair in cot_own], axis=0).astype(F32)
        cot_near = swap_y(cot_mine)
        cot_near = rounded(cot_near, swap_core(cot_near), 0)
        got = [swap_y(own) for own in middle_own]
        got_other = [swap_core(value) for value in got]
        middle_near = jnp.concatenate(got + got_other, axis=0)
        _, _, normed_near, hidden_near, d_gate_near, d_up_near = glu(
            middle_near, right_dot(cot_near, w_down)
        )
        both_cot = jnp.concatenate([cot_rows, cot_near], axis=0)
        both_normed = jnp.concatenate([normed_two, normed_near], axis=0)
        both_hidden = jnp.concatenate([hidden, hidden_near], axis=0)
        both_gate = jnp.concatenate([d_gate, d_gate_near], axis=0)
        both_up = jnp.concatenate([d_up, d_up_near], axis=0)
        block = width // 8

        def features(value, q):
            return lax.dynamic_slice_in_dim(value, q * 2 * block + side * block, block, 1)

        grad_w_down = chain(lambda q: left_dot(both_hidden, features(both_cot, q)))
        grad_w_gate = chain(lambda q: left_dot(features(both_normed, q), both_gate))
        grad_w_up = chain(lambda q: left_dot(features(both_normed, q), both_up))

        def near_half(value, order):
            value, _ = lax.optimization_barrier((value, order))
            columns = side_columns(value, 1 - side)
            h = rows // 2
            own = lax.dynamic_slice_in_dim(columns, core * h, h, 0)
            own = swap_y(own)
            return rounded(own, swap_core(own), core)

        one_near = near_half(normed_one_wide, middle_near)
        branch_near = near_half(d_branch_wide, middle_near)

        def near(value):
            value = swap_y(value)
            return rounded(value[: rows // 2], value[rows // 2 :], 0)

        gated_near = near(after(gated_wide, middle_near))
        joined = jnp.concatenate([d_input_wide, d_pforget_wide, d_rgate_wide], axis=1)
        joined_near = near(joined)
        both_joined = jnp.concatenate([joined.astype(BF16), joined_near], axis=0)
        both_one = jnp.concatenate([side_columns(normed_one, side), one_near], axis=0)
        both_branch = jnp.concatenate([side_columns(d_branch, side), branch_near], axis=0)
        both_gated = jnp.concatenate([gated, gated_near], axis=0)

        def own_features(value, q):
            return lax.dynamic_slice_in_dim(value, q * block, block, 1)

        grad_w_out = chain(lambda q: left_dot(both_gated, own_features(both_branch, q)))
        grad_joined = chain(lambda q: left_dot(own_features(both_one, q), both_joined))
        grads = (
            grad_joined[:, :channels],
            grad_joined[:, channels : 2 * channels],
            grad_joined[:, 2 * channels :],
            grad_w_out,
            grad_w_gate,
            grad_w_up,
            grad_w_down,
        )

    return (
        mixed_out,
        grad_tokens,
        grad_attn,
        grads[0],
        grads[1],
        grads[2],
        grad_gnorm,
        grad_bound,
        grads[3],
        grad_mlp,
        grads[4],
        grads[5],
        grads[6],
    )


def solution(mesh):
    in_specs = (
        P("seq", None),
        P(),
        P(None, "mp"),
        P(None, "mp"),
        P(None, "mp"),
        P("mp"),
        P("mp"),
        P("mp", None),
        P(),
        P(None, "mp"),
        P(None, "mp"),
        P("mp", None),
        P("seq", None),
        P("seq", None),
    )
    out_specs = (
        P("seq", None),
        P("seq", None),
        P("seq"),
        P("seq", "mp"),
        P("seq", "mp"),
        P("seq", "mp"),
        P("mp", "seq"),
        P("mp", "seq"),
        P("mp", "seq"),
        P("seq"),
        P("seq", "mp"),
        P("seq", "mp"),
        P("mp", "seq"),
    )
    return jax.shard_map(
        per_device, mesh=mesh, in_specs=in_specs, out_specs=out_specs, check_vma=False
    )
```

```python
import jax
import jax.numpy as jnp
from jax import lax
from jax.experimental import pallas as pl
from jax.experimental.pallas import tpu as pltpu
from jax.sharding import PartitionSpec as P

LCHUNK = 256
norm_eps = 1e-06
FL = {'cot': (0,), 'cot_ready': (0, 1), 'prefix': (0,), 'glu': (), 'branch': (), 'inner': (0,), 'feed': (1,), 'one': (), 'one_ready': (0,), 'gated': (), 'gated_ready': (0,), 'kernel': 0, 'kernel_rec': 0, 'gate': (0,), 'far_down': (0,), 'far_gate': (), 'far_up': (0,), 'joined': (), 'near_branch': (), 'branch_ready': (), 'out': (), 'far_joined': (), 'far_out': (), 'own_down': (2,), 'own_gate': (2,), 'own_up': (2,), 'own_joined': (), 'own_out': (), 'end_down': (1, 2), 'end_gate': (1, 2), 'end_up': (1, 2), 'end_joined': (), 'end_out': (), 'sends': 7, 'direct': 0, 'steps': (1, 2, 4)}
F32 = jnp.float32
BF16 = jnp.bfloat16

CORE_PAIRS = [(i, i ^ 1) for i in range(4)]
X_PAIRS = [(i, i ^ 2) for i in range(4)]
Y_PAIRS = [(i, i ^ 1) for i in range(8)]
Z_PAIRS = [(i, i ^ 2) for i in range(8)]
FAR_PAIRS = [(i, i ^ 4) for i in range(8)]


def dot(left, right):
    return jnp.dot(left, right, preferred_element_type=F32)


def left_dot(left, right):
    return lax.dot_general(left, right, (((0,), (0,)), ((), ())), preferred_element_type=F32)


def right_dot(left, right):
    return lax.dot_general(left, right, (((1,), (1,)), ((), ())), preferred_element_type=F32)


def silu_slope(values):
    sig = jax.nn.sigmoid(values)
    return sig * (1.0 + values * (1.0 - sig))


def pick(name, options):
    return [options[i] for i in FL[name]]


def spark(*others):
    firsts = [
        lax.reshape(lax.slice(other, (0,) * other.ndim, (1,) * other.ndim), ()).astype(F32)
        for other in others
    ]
    return sum(firsts) * 0.0


def after(value, *others):
    return value + spark(*others) if others else value


def later(index, *others):
    return index + spark(*others).astype(jnp.int32) if others else index


def place_kernel(moves, flip_ref, *refs):
    out_ref = refs[-1]
    for flip, plan in enumerate(moves):

        @pl.when((flip_ref[0] != 0) == bool(flip))
        def _():
            for index, source, size, target in plan:
                out_ref[target : target + size, :] = refs[index][source : source + size, :].astype(
                    BF16
                )


def placed(values, rows, plan, other_plan=None, flip=0):
    width = values[0].shape[1]
    block = 256
    moves = (plan,) if other_plan is None else (plan, other_plan)
    return pl.pallas_call(
        lambda *refs: place_kernel(moves, *refs),
        grid=(width // block,),
        in_specs=[pl.BlockSpec(memory_space=pltpu.SMEM)]
        + [pl.BlockSpec((value.shape[0], block), lambda i: (0, i)) for value in values],
        out_specs=pl.BlockSpec((rows, block), lambda i: (0, i)),
        out_shape=jax.ShapeDtypeStruct((rows, width), BF16),
        compiler_params=pltpu.CompilerParams(vmem_limit_bytes=24 * 1024 * 1024),
        cost_estimate=pl.CostEstimate(
            flops=rows * width, bytes_accessed=rows * width * 6, transcendentals=0
        ),
        name="placed",
    )(jnp.full((1,), flip, jnp.int32), *values)


def norm_kernel(gain_ref, *refs):
    out_ref = refs[-1]
    target = 0
    for ref in refs[:-1]:
        values = ref[...]
        scale = lax.rsqrt(jnp.mean(values * values, axis=1, keepdims=True) + norm_eps)
        size = values.shape[0]
        out_ref[target : target + size, :] = (values * scale * gain_ref[...]).astype(BF16)
        target += size


def normed_rows(values, gain):
    width = gain.shape[0]
    rows = sum(value.shape[0] for value in values)
    return pl.pallas_call(
        norm_kernel,
        out_shape=jax.ShapeDtypeStruct((rows, width), BF16),
        compiler_params=pltpu.CompilerParams(vmem_limit_bytes=32 * 1024 * 1024),
        cost_estimate=pl.CostEstimate(
            flops=rows * width * 5, bytes_accessed=rows * width * 6, transcendentals=rows
        ),
        name="normed_rows",
    )(gain[None, :], *values)


def block_kernel(depth, at_ref, left_ref, right_ref, *refs):
    out_ref = refs[-1]
    step = pl.program_id(0)
    product = lax.dot_general(
        left_ref[...], right_ref[...], (((0,), (0,)), ((), ())), preferred_element_type=F32
    )

    @pl.when(step == 0)
    def _():
        total = product
        for ref in refs[:-1]:
            total += ref[...]
        out_ref[...] = total

    @pl.when(step > 0)
    def _():
        out_ref[...] += product


def block_product(left, left_at, right, right_at, *adds):
    block = 256
    rows = left.shape[0]
    steps = 3
    depth = rows // steps
    height = left.shape[1] if left_at is None else block
    width = right.shape[1] if right_at is None else block
    at = jnp.stack([jnp.int32(0) if p is None else p for p in (left_at, right_at)])

    def spec(wide, which, picked):
        def place(step, at_ref):
            return step, (at_ref[which] if picked else 0)

        return pl.BlockSpec((depth, wide), place)

    whole = pl.BlockSpec((height, width), lambda step, at_ref: (0, 0))
    return pl.pallas_call(
        lambda *refs: block_kernel(depth, *refs),
        grid_spec=pltpu.PrefetchScalarGridSpec(
            num_scalar_prefetch=1,
            grid=(steps,),
            in_specs=[
                spec(height, 0, left_at is not None),
                spec(width, 1, right_at is not None),
                *[whole] * len(adds),
            ],
            out_specs=whole,
        ),
        out_shape=jax.ShapeDtypeStruct((height, width), F32),
        compiler_params=pltpu.CompilerParams(vmem_limit_bytes=32 * 1024 * 1024),
        name="block_product",
    )(at, left, right, *adds)


def group_scan(a, b, backward):
    place = lax.broadcasted_iota(jnp.int32, a.shape, 0)
    for step in (1, 2, 4):
        shift = 8 - step if backward else step
        inside = place < 8 - step if backward else place >= step
        a_shift = jnp.where(inside, pltpu.roll(a, shift, 0), 1.0)
        b_shift = jnp.where(inside, pltpu.roll(b, shift, 0), 0.0)
        b = a * b_shift + b
        a = a * a_shift
    return a, b


def forth_kernel(a_ref, b_ref, x_ref, p_ref, before_ref, p_before_ref):
    rows, width = a_ref.shape
    first = lax.broadcasted_iota(jnp.int32, (8, width), 0) == 0

    def last(value):
        return jnp.broadcast_to(value[7:8, :], (8, width))

    def run(begin, count, long):
        def body(step, carry):
            carry_x, carry_p = carry
            here = pl.ds(pl.multiple_of(begin + step * 8, 8), 8)
            decay = a_ref[here, :]
            a, b = group_scan(decay, b_ref[here, :], False)
            x = b + a * carry_x
            x_ref[here, :] = x
            before = jnp.where(first, carry_x, pltpu.roll(x, 1, 0))
            before_ref[here, :] = jnp.where(decay == 0.0, 0.0, before)
            if long:
                product = a * carry_p
                p_ref[here, :] = product
                p_before_ref[here, :] = jnp.where(first, carry_p, pltpu.roll(product, 1, 0))
                carry_p = last(product)
            return last(x), carry_p

        start = (jnp.zeros((8, width), F32), jnp.ones((8, width), F32))
        lax.fori_loop(0, count, body, start, unroll=4)

    run(0, LCHUNK // 8, True)
    run(LCHUNK, (rows - LCHUNK) // 8, False)


def back_kernel(a_ref, b_ref, x_ref, p_ref):
    rows, width = a_ref.shape
    end = lax.broadcasted_iota(jnp.int32, (8, width), 0) == 7

    def top(value):
        return jnp.broadcast_to(value[0:1, :], (8, width))

    def run(begin, count, long):
        def body(step, carry):
            carry_x, carry_p, carry_a = carry
            here = pl.ds(pl.multiple_of(begin + (count - 1 - step) * 8, 8), 8)
            decay = a_ref[here, :]
            link = jnp.where(end, carry_a, pltpu.roll(decay, 7, 0))
            a, b = group_scan(link, b_ref[here, :], True)
            x = b + a * carry_x
            x_ref[here, :] = x
            if long:
                product = a * carry_p
                p_ref[here, :] = product
                carry_p = top(product)
            return top(x), carry_p, top(decay)

        one = jnp.ones((8, width), F32)
        lax.fori_loop(0, count, body, (jnp.zeros((8, width), F32), one, one), unroll=4)

    run(0, LCHUNK // 8, True)
    run(LCHUNK, (rows - LCHUNK) // 8, False)


def scan(a, b, backward):
    rows, width = a.shape
    block = 256
    spec = pl.BlockSpec((rows, block), lambda i: (0, i))
    long_spec = pl.BlockSpec((LCHUNK, block), lambda i: (0, i))
    shape = jax.ShapeDtypeStruct((rows, width), F32)
    long_shape = jax.ShapeDtypeStruct((LCHUNK, width), F32)
    times = 1 if backward else 2
    return pl.pallas_call(
        back_kernel if backward else forth_kernel,
        grid=(width // block,),
        in_specs=[spec, spec],
        out_specs=[spec, long_spec] * times,
        out_shape=[shape, long_shape] * times,
        compiler_params=pltpu.CompilerParams(vmem_limit_bytes=24 * 1024 * 1024),
        cost_estimate=pl.CostEstimate(
            flops=rows * width * 12, bytes_accessed=rows * width * 14, transcendentals=0
        ),
        name="scan_back" if backward else "scan_forth",
    )(a, b)


def carry_of(decay, local, backward, *before):
    count, mine = lax.axis_size("seq"), lax.axis_index("seq")
    ends = jnp.stack([decay, local])
    if count != 8:
        pieces = lax.all_gather(ends, "seq")
        order = jnp.arange(count)
        total = jnp.zeros_like(local)
        for step in range(count):
            i = count - 1 - step if backward else step
            use = (order[i] > mine) if backward else (order[i] < mine)
            total = jnp.where(use, pieces[i, 0] * total + pieces[i, 1], total)
        return total, total
    partner = lax.ppermute(ends, "seq", Y_PAIRS)
    first = (mine % 2 == 1) if backward else (mine % 2 == 0)
    early = jnp.where(first, ends, partner)
    late = jnp.where(first, partner, ends)
    pair = after(jnp.stack([early[0] * late[0], late[0] * early[1] + late[1]]), *before)
    total = jnp.zeros_like(local)
    got = []
    for hops in (3, 2, 1):
        if backward:
            pairs = [(i + 2 * hops, i) for i in range(8 - 2 * hops)]
        else:
            pairs = [(i, i + 2 * hops) for i in range(8 - 2 * hops)]
        got.append(lax.ppermute(pair, "seq", pairs))
    for piece in got:
        total = piece[0] * total + piece[1]
    return jnp.where(first, total, partner[0] * total + partner[1]), partner


def small_psum(value):
    value = value + lax.ppermute(value, "mp", CORE_PAIRS)
    return value + lax.ppermute(value, "mp", X_PAIRS)


def summed_half(send, keep):
    value = keep + lax.ppermute(send, "mp", CORE_PAIRS)
    return value + lax.ppermute(value, "mp", X_PAIRS), value


def per_device(
    tokens,
    attn_gain,
    w_input,
    w_forget,
    w_rgate,
    gnorm_gain,
    lower_bound,
    w_out,
    mlp_gain,
    w_gate,
    w_up,
    w_down,
    local_lengths,
    cotangent,
):
    rows, width = tokens.shape
    short_rows = rows - LCHUNK
    count, mine = lax.axis_size("seq"), lax.axis_index("seq")
    fast = count == 8
    core = lax.axis_index("mp") % 2
    side = mine % 2
    chunks = ((LCHUNK, short_rows), (0, LCHUNK))

    def half(value, own, chunk):
        first, size = chunk
        which = core if own else 1 - core
        return lax.dynamic_slice_in_dim(value, first + which * (size // 2), size // 2, 0)

    def swap_core(value):
        return lax.ppermute(value, "mp", CORE_PAIRS)

    def swap_y(value):
        return lax.ppermute(value, "seq", Y_PAIRS)

    def canonical(parts):
        out = []
        for own, other in (parts[1], parts[0]):
            out.append(jnp.where(core == 0, own, other))
            out.append(jnp.where(core == 0, other, own))
        return jnp.concatenate(out, axis=0)

    lengths_row = local_lengths[0]
    offsets = jnp.cumsum(lengths_row) - lengths_row
    starts = jnp.any(
        jnp.arange(short_rows, dtype=jnp.int32)[:, None] == offsets[None, :], axis=1
    )[:, None]

    sizes = [size // 2 for _, size in chunks]
    cot_own = [(half(cotangent, True, c), half(cotangent, False, c)) for c in chunks]

    def near_rows(value, *ready):
        own = after(lax.ppermute(value, "seq", Z_PAIRS), *ready)
        return [own, swap_core(own)]

    def near_cot(index, *before):
        value = near_rows(
            after(cot_own[index][0].astype(F32), *before),
            *pick("cot_ready", (middle_own[0], middle_own[1])),
        )
        h = sizes[index]
        return placed(value, 2 * h, [(0, 0, h, 0), (1, 0, h, h)])

    if fast:
        near_cots = [None, None]

    stream = tokens.astype(F32)
    first_gain = attn_gain.astype(F32)
    first_scale = lax.rsqrt(jnp.mean(stream * stream, axis=1, keepdims=True) + norm_eps)
    normed_one_wide = stream * first_scale * first_gain
    normed_one = normed_one_wide.astype(BF16)
    pre_forget = dot(normed_one, w_forget)
    pre_input = dot(normed_one, w_input)
    pre_rgate = dot(normed_one, w_rgate)
    forget_sig = jax.nn.sigmoid(pre_forget)
    forget = lower_bound + (1.0 - lower_bound) * forget_sig
    input_act = jax.nn.silu(pre_input)
    drive = input_act * (1.0 - forget)
    is_start = jnp.concatenate([jnp.zeros((LCHUNK, 1), bool), starts], axis=0)
    decay = jnp.where(is_start, 0.0, forget)
    states_local, long_decay, before_local, before_decay = scan(decay, drive, False)

    def entered(local, product, carry):
        return jnp.concatenate(
            [local[:LCHUNK] + product * carry[None, :], local[LCHUNK:]], axis=0
        )

    state_gain = gnorm_gain.astype(F32)
    rgate_act = jax.nn.silu(pre_rgate)
    second_gain = mlp_gain.astype(F32)

    def row_scale(values):
        return lax.rsqrt(jnp.mean(values * values, axis=1, keepdims=True) + norm_eps)

    def glu(normed, d_hid):
        gate = dot(normed, w_gate)
        up = dot(normed, w_up)
        act = jax.nn.silu(gate)
        hidden = (act * up).astype(BF16)
        d_gate = (d_hid * up * silu_slope(gate)).astype(BF16)
        d_up = (d_hid * act).astype(BF16)
        return hidden, d_gate, d_up

    states_of, scale_of, gated_of, middle_own, middle_other = [], [], [], [], []
    for index, (first, size) in enumerate(chunks):
        local = states_local[first : first + size]
        if index == 1:
            carry_in, _ = carry_of(
                long_decay[-1], states_local[LCHUNK - 1], False, *pick("prefix", (short_sent,))
            )
            local = local + long_decay * carry_in[None, :]
        squares = small_psum(jnp.sum(local * local, axis=1))
        scale = lax.rsqrt(squares / width + norm_eps)[:, None]
        gated = local * scale * state_gain * rgate_act[first : first + size]
        gated16 = gated.astype(BF16)
        states_of.append(local)
        scale_of.append(scale)
        gated_of.append(gated)
        h = size // 2
        send = dot(lax.dynamic_slice_in_dim(gated16, (1 - core) * h, h, 0), w_out)
        keep = dot(lax.dynamic_slice_in_dim(gated16, core * h, h, 0), w_out)
        if index == 0:
            short_sent = send
        total, kept = summed_half(send, keep)
        own = half(tokens, True, (first, size)).astype(F32) + total
        middle_own.append(own)
        middle_other.append(swap_core(own))

    if fast:
        near_cots = [near_cot(i, *pick("cot", (carry_in, short_sent))) for i in (0, 1)]
    cot_rows = jnp.concatenate(
        [part for pair in cot_own for part in pair], axis=0
    )
    d_hidden = right_dot(cot_rows, w_down)
    states = jnp.concatenate([states_of[1], states_of[0]], axis=0)
    state_scale = jnp.concatenate([scale_of[1], scale_of[0]], axis=0)
    gated_wide = jnp.concatenate([gated_of[1], gated_of[0]], axis=0)
    gated = gated_wide.astype(BF16)
    normed_state = states * state_scale

    offset = 0
    main, d_mid_own, d_mid_other, hat_grad, feeds = [], [], [], [], []
    for index, (first, size) in enumerate(chunks):
        h = size // 2
        middle = jnp.concatenate([middle_own[index], middle_other[index]], axis=0)
        scale = row_scale(middle)
        hat = middle * scale
        normed = (hat * second_gain).astype(BF16)
        hidden, d_gate, d_up = glu(normed, d_hidden[offset : offset + size])
        offset += size
        main.append((normed, hidden, d_gate, d_up))
        send = right_dot(d_gate[h:], w_gate) + right_dot(d_up[h:], w_up)
        keep = right_dot(d_gate[:h], w_gate) + right_dot(d_up[:h], w_up)
        d_normed, glu_kept = summed_half(send, keep)
        hat, scale = hat[:h], scale[:h]
        hat_grad.append(jnp.sum(d_normed * hat, axis=0))
        e = d_normed * second_gain
        turn = scale * (e - hat * jnp.mean(e * hat, axis=1, keepdims=True))
        d_mid_own.append(cot_own[index][0].astype(F32) + turn)
        d_mid_other.append(cot_own[index][1].astype(F32) + swap_core(turn))

    normed_two, hidden, d_gate, d_up = (
        jnp.concatenate([main[0][i], main[1][i]], axis=0) for i in range(4)
    )

    if fast:
        sets = [(cot_rows, normed_two, hidden, d_gate, d_up)]
        for own, cot in zip(middle_own, near_cots):
            normed = normed_rows(near_rows(own), after(second_gain, *pick("glu", (glu_kept,))))
            sets.append((cot, normed, *glu(normed, right_dot(cot, w_down))))
        arrived = sets[-1][1]
        cots, normed, hiddens, gates, ups = (
            jnp.concatenate(parts, axis=0) for parts in zip(*sets)
        )
        block = width // 8
        plane = mine // 2
        planes = (plane, jnp.bitwise_xor(plane, 2))
        h = rows // 2

        def columns(value, start):
            return lax.dynamic_slice_in_dim(value, start * block, block, 1)

        def part_down(i, y):
            return left_dot(hiddens, columns(cots, 2 * planes[i] + y))

        down_sent = part_down(1, 1 - side)
        down_got = swap_y(down_sent)

    d_branch_wide = canonical(list(zip(d_mid_own, d_mid_other)))
    if fast:
        d_branch_wide = after(d_branch_wide, *pick("branch", (down_sent, down_got)))
    d_branch = d_branch_wide.astype(BF16)
    d_gated = right_dot(d_branch, w_out)
    grad_gnorm = jnp.sum(d_gated * normed_state * rgate_act, axis=0)
    d_rgate_wide = d_gated * normed_state * state_gain * silu_slope(pre_rgate)
    d_normed = d_gated * state_gain * rgate_act
    inner = small_psum(jnp.sum(d_normed * normed_state, axis=1))
    d_normed_last = d_mid_own[1]
    for index, (first, size) in enumerate(chunks):
        size = size // 2
        start = later(0, *pick("feed", (d_normed_last, inner)))
        feeds.append(
            [
                dot(lax.dynamic_slice_in_dim(main[index][1], start + i * size, size, 0), w_down)
                for i in (1, 0)
            ]
        )
    if fast:
        inner = after(inner, *pick("inner", (down_got,)))
    d_states = state_scale * (d_normed - normed_state * (inner / width)[:, None])
    back_local, back_decay = scan(decay, d_states, True)
    carried_in, carry_sent = carry_of(forget[0] * back_decay[0], forget[0] * back_local[0], True)
    carried = entered(back_local, back_decay, carried_in)
    states_prev = entered(before_local, before_decay, carry_in)
    d_forget = carried * (states_prev - input_act)
    d_input_wide = carried * (1.0 - forget) * silu_slope(pre_input)
    d_pforget_wide = d_forget * (1.0 - lower_bound) * forget_sig * (1.0 - forget_sig)
    grad_bound = jnp.sum(d_forget * (1.0 - forget_sig), axis=0)
    d_input = d_input_wide.astype(BF16)
    d_pforget = d_pforget_wide.astype(BF16)
    d_rgate = d_rgate_wide.astype(BF16)

    d_stream, first_grad = [], []
    for index, chunk in enumerate(chunks):
        both = []
        for own in (False, True):
            both.append(
                right_dot(half(d_input, own, chunk), w_input)
                + right_dot(half(d_pforget, own, chunk), w_forget)
                + right_dot(half(d_rgate, own, chunk), w_rgate)
            )
        d_normed_one, _ = summed_half(*both)
        part = half(tokens, True, chunk).astype(F32)
        scale = row_scale(part)
        hat = part * scale
        first_grad.append(jnp.sum(d_normed_one * hat, axis=0))
        e = d_normed_one * first_gain
        turn = scale * (e - hat * jnp.mean(e * hat, axis=1, keepdims=True))
        d_stream.append((d_mid_own[index] + turn, d_mid_other[index] + swap_core(turn)))
    grad_tokens = canonical(d_stream).astype(BF16)

    mixed = []
    for own, other, feed in zip(middle_own, middle_other, feeds):
        value, _ = summed_half(*feed)
        mixed.append((own + value, other + swap_core(value)))
    mixed_out = canonical(mixed).astype(BF16)

    channels = grad_gnorm.shape[0]
    sends = []
    if not fast:

        def scattered(value, dim):
            return lax.psum_scatter(value, "seq", scatter_dimension=dim, tiled=True)

        grads = (
            scattered(left_dot(normed_one, d_input), 0),
            scattered(left_dot(normed_one, d_pforget), 0),
            scattered(left_dot(normed_one, d_rgate), 0),
            scattered(left_dot(gated, d_branch), 1),
            scattered(left_dot(normed_two, d_gate), 0),
            scattered(left_dot(normed_two, d_up), 0),
            scattered(left_dot(hidden, cot_rows), 1),
        )
    else:
        def near_columns(value, before, *ready):
            parts = [
                lax.dynamic_slice(
                    value,
                    (later(core * h, *before), 2 * jnp.bitwise_xor(q, 1) * block),
                    (h, 2 * block),
                )
                for q in planes
            ]
            low, high = [(0, 0, h, 0), (1, 0, h, h)], [(0, 0, h, h), (1, 0, h, 0)]
            return placed(near_rows(jnp.concatenate(parts, axis=1)), rows, low, high, later(core, *ready))

        def near_whole(value, *ready):
            near = lax.ppermute(value, "seq", Z_PAIRS)
            return placed([near], rows, [(0, 0, rows, 0)], flip=later(0, *ready))

        def pair_columns(value):
            return jnp.concatenate(
                [lax.dynamic_slice_in_dim(value, 2 * q * block, 2 * block, 1) for q in planes],
                axis=1,
            )

        joined_wide = jnp.concatenate([d_input_wide, d_pforget_wide, d_rgate_wide], axis=1)
        near_one = near_columns(
            normed_one_wide, pick("one", (arrived, carried_in)), *pick("one_ready", (joined_wide,))
        )
        near_gated = near_whole(
            after(gated_wide, *pick("gated", (arrived, carried_in))),
            *pick("gated_ready", (joined_wide,)),
        )

        def mm(kind, left, left_at, right, right_at):
            if FL[kind]:
                return block_product(left, left_at, right, right_at)
            left = left if left_at is None else columns(left, left_at)
            right = right if right_at is None else columns(right, right_at)
            return left_dot(left, right)

        def part_gate(i, y):
            return mm("kernel", normed, 2 * planes[i] + y, gates, None)

        def part_up(i, y):
            return mm("kernel", normed, 2 * planes[i] + y, ups, None)

        def part_out(i, y):
            return mm("kernel_rec", both_gated, None, both_branch, 2 * i + y)

        def part_joined(i, y):
            return mm("kernel_rec", both_one, 2 * i + y, joined, None)

        def swap_far(value):
            return lax.ppermute(value, "seq", FAR_PAIRS)

        gate_sent = part_gate(1, later(1 - side, *pick("gate", (carry_sent,))))
        up_sent = part_up(1, later(1 - side, *pick("gate", (carry_sent,))))
        far_down = part_down(1, later(side, *pick("far_down", (carry_sent, carried_in)))) + down_got
        far_gate = part_gate(1, later(side, *pick("far_gate", (carried_in, joined_wide)))) + swap_y(gate_sent)
        far_up = part_up(1, later(side, *pick("far_up", (carried_in, joined_wide, far_gate)))) + swap_y(up_sent)
        far_down_got, far_gate_got, far_up_got = (
            swap_far(value) for value in (far_down, far_gate, far_up)
        )
        near_joined = near_whole(
            joined_wide, *pick("joined", (far_down_got, far_gate_got, far_up, far_down))
        )
        near_branch = near_columns(
            d_branch_wide, pick("near_branch", (joined_wide, far_up)), *pick("branch_ready", (near_joined,))
        )
        mine_joined = jnp.concatenate([d_input, d_pforget, d_rgate], axis=1)
        joined = jnp.concatenate([mine_joined, near_joined], axis=0)
        both_one = jnp.concatenate([pair_columns(normed_one), near_one], axis=0)
        both_branch = jnp.concatenate([pair_columns(d_branch), near_branch], axis=0)
        both_gated = jnp.concatenate([gated, near_gated], axis=0)

        joined_sent = part_joined(1, 1 - side)
        out_sent = part_out(1, later(1 - side, *pick("out", (joined_sent,))))
        far_joined = part_joined(1, later(side, *pick("far_joined", (far_up_got, far_gate_got)))) + swap_y(
            joined_sent
        )
        far_out = part_out(1, later(side, *pick("far_out", (far_joined,)))) + swap_y(out_sent)

        def finish(part, got, name):
            sent = part(0, later(1 - side, *pick("own_" + name, (up_sent, joined_sent, far_joined))))
            kept = part(0, later(side, *pick("end_" + name, (joined_sent, far_joined, far_out))))
            ends.append(sent)
            return kept + swap_y(sent) + got

        ends = [far_joined, far_out]
        grad_w_down = finish(part_down, far_down_got, "down")
        grad_w_gate = finish(part_gate, far_gate_got, "gate")
        grad_w_up = finish(part_up, far_up_got, "up")
        grad_joined = finish(part_joined, swap_far(far_joined), "joined")
        grad_w_out = finish(part_out, swap_far(far_out), "out")
        sends = ends[: FL["sends"]]
        grads = (
            grad_joined[:, :channels],
            grad_joined[:, channels : 2 * channels],
            grad_joined[:, 2 * channels :],
            grad_w_out,
            grad_w_gate,
            grad_w_up,
            grad_w_down,
        )

    rowsum = jnp.stack([sum(first_grad), sum(hat_grad)])
    rowsum = rowsum + swap_core(rowsum)
    pieces = jnp.concatenate(
        [
            rowsum.reshape(2, count, width // count).transpose(1, 0, 2).reshape(count, -1),
            grad_gnorm.reshape(count, -1),
            grad_bound.reshape(count, -1),
        ],
        axis=1,
    )
    if not fast:
        vectors = lax.psum_scatter(pieces, "seq", scatter_dimension=0, tiled=True)[0]
    elif FL["direct"]:
        pieces = after(pieces, *sends)
        vectors = lax.dynamic_index_in_dim(pieces, mine, 0, keepdims=False)
        for step in range(1, 8):
            piece = lax.dynamic_index_in_dim(pieces, jnp.bitwise_xor(mine, step), 0, keepdims=False)
            vectors += lax.ppermute(piece, "seq", [(i, i ^ step) for i in range(8)])
    else:
        pieces = after(pieces, *sends)
        for step in FL["steps"]:
            pieces = pieces + lax.ppermute(pieces, "seq", [(i, i ^ step) for i in range(8)])
        vectors = lax.dynamic_index_in_dim(pieces, mine, 0, keepdims=False)
    part, small = width // count, channels // count
    grad_attn, grad_mlp = vectors[:part], vectors[part : 2 * part]
    grad_gnorm = vectors[2 * part : 2 * part + small][None, :]
    grad_bound = vectors[2 * part + small :][None, :]

    return (
        mixed_out,
        grad_tokens,
        grad_attn,
        grads[0],
        grads[1],
        grads[2],
        grad_gnorm,
        grad_bound,
        grads[3],
        grad_mlp,
        grads[4],
        grads[5],
        grads[6],
    )


def solution(mesh):
    in_specs = (
        P("seq", None),
        P(),
        P(None, "mp"),
        P(None, "mp"),
        P(None, "mp"),
        P("mp"),
        P("mp"),
        P("mp", None),
        P(),
        P(None, "mp"),
        P(None, "mp"),
        P("mp", None),
        P("seq", None),
        P("seq", None),
    )
    out_specs = (
        P("seq", None),
        P("seq", None),
        P("seq"),
        P("seq", "mp"),
        P("seq", "mp"),
        P("seq", "mp"),
        P("mp", "seq"),
        P("mp", "seq"),
        P("mp", "seq"),
        P("seq"),
        P("seq", "mp"),
        P("seq", "mp"),
        P("mp", "seq"),
    )
    return jax.shard_map(
        per_device, mesh=mesh, in_specs=in_specs, out_specs=out_specs, check_vma=False
    )
```

```python
import jax
import jax.numpy as jnp
from jax import lax
from jax.experimental import pallas as pl
from jax.experimental.pallas import tpu as pltpu
from jax.sharding import PartitionSpec as P

LCHUNK = 256
norm_eps = 1e-06
FL = {'cot': (0,), 'cot_ready': (0, 1), 'prefix': (0,), 'glu': (), 'branch': (), 'inner': (0,), 'feed': (0,), 'one': (), 'one_ready': (0,), 'gated': (), 'gated_ready': (0,), 'kernel': 0, 'kernel_rec': 0, 'gate': (0,), 'far_down': (0,), 'far_gate': (), 'far_up': (0,), 'joined': (0,), 'near_branch': (), 'branch_ready': (), 'out': (0,), 'far_joined': (1,), 'far_out': (), 'own_down': (1,), 'own_gate': (2,), 'own_up': (2,), 'own_joined': (), 'own_out': (2,), 'end_down': (1, 2), 'end_gate': (0,), 'end_up': (1, 2), 'end_joined': (), 'end_out': (1,), 'sends': 2, 'direct': 0, 'steps': (2, 1, 4), 'dn1': (), 'carried': (), 'suffix': ()}
F32 = jnp.float32
BF16 = jnp.bfloat16

CORE_PAIRS = [(i, i ^ 1) for i in range(4)]
X_PAIRS = [(i, i ^ 2) for i in range(4)]
Y_PAIRS = [(i, i ^ 1) for i in range(8)]
Z_PAIRS = [(i, i ^ 2) for i in range(8)]
FAR_PAIRS = [(i, i ^ 4) for i in range(8)]


def dot(left, right):
    return jnp.dot(left, right, preferred_element_type=F32)


def left_dot(left, right):
    return lax.dot_general(left, right, (((0,), (0,)), ((), ())), preferred_element_type=F32)


def right_dot(left, right):
    return lax.dot_general(left, right, (((1,), (1,)), ((), ())), preferred_element_type=F32)


def silu_slope(values):
    sig = jax.nn.sigmoid(values)
    return sig * (1.0 + values * (1.0 - sig))


def pick(name, options):
    return [options[i] for i in FL[name]]


def spark(*others):
    firsts = [
        lax.reshape(lax.slice(other, (0,) * other.ndim, (1,) * other.ndim), ()).astype(F32)
        for other in others
    ]
    return sum(firsts) * 0.0


def after(value, *others):
    return value + spark(*others) if others else value


def later(index, *others):
    return index + spark(*others).astype(jnp.int32) if others else index


def place_kernel(moves, flip_ref, *refs):
    out_ref = refs[-1]
    for flip, plan in enumerate(moves):

        @pl.when((flip_ref[0] != 0) == bool(flip))
        def _():
            for index, source, size, target in plan:
                out_ref[target : target + size, :] = refs[index][source : source + size, :].astype(
                    BF16
                )


def placed(values, rows, plan, other_plan=None, flip=0):
    width = values[0].shape[1]
    block = 256
    moves = (plan,) if other_plan is None else (plan, other_plan)
    return pl.pallas_call(
        lambda *refs: place_kernel(moves, *refs),
        grid=(width // block,),
        in_specs=[pl.BlockSpec(memory_space=pltpu.SMEM)]
        + [pl.BlockSpec((value.shape[0], block), lambda i: (0, i)) for value in values],
        out_specs=pl.BlockSpec((rows, block), lambda i: (0, i)),
        out_shape=jax.ShapeDtypeStruct((rows, width), BF16),
        compiler_params=pltpu.CompilerParams(vmem_limit_bytes=24 * 1024 * 1024),
        cost_estimate=pl.CostEstimate(
            flops=rows * width, bytes_accessed=rows * width * 6, transcendentals=0
        ),
        name="placed",
    )(jnp.full((1,), flip, jnp.int32), *values)


def norm_kernel(gain_ref, *refs):
    out_ref = refs[-1]
    target = 0
    for ref in refs[:-1]:
        values = ref[...]
        scale = lax.rsqrt(jnp.mean(values * values, axis=1, keepdims=True) + norm_eps)
        size = values.shape[0]
        out_ref[target : target + size, :] = (values * scale * gain_ref[...]).astype(BF16)
        target += size


def normed_rows(values, gain):
    width = gain.shape[0]
    rows = sum(value.shape[0] for value in values)
    return pl.pallas_call(
        norm_kernel,
        out_shape=jax.ShapeDtypeStruct((rows, width), BF16),
        compiler_params=pltpu.CompilerParams(vmem_limit_bytes=32 * 1024 * 1024),
        cost_estimate=pl.CostEstimate(
            flops=rows * width * 5, bytes_accessed=rows * width * 6, transcendentals=rows
        ),
        name="normed_rows",
    )(gain[None, :], *values)


def block_kernel(depth, at_ref, left_ref, right_ref, *refs):
    out_ref = refs[-1]
    step = pl.program_id(0)
    product = lax.dot_general(
        left_ref[...], right_ref[...], (((0,), (0,)), ((), ())), preferred_element_type=F32
    )

    @pl.when(step == 0)
    def _():
        total = product
        for ref in refs[:-1]:
            total += ref[...]
        out_ref[...] = total

    @pl.when(step > 0)
    def _():
        out_ref[...] += product


def block_product(left, left_at, right, right_at, *adds):
    block = 256
    rows = left.shape[0]
    steps = 3
    depth = rows // steps
    height = left.shape[1] if left_at is None else block
    width = right.shape[1] if right_at is None else block
    at = jnp.stack([jnp.int32(0) if p is None else p for p in (left_at, right_at)])

    def spec(wide, which, picked):
        def place(step, at_ref):
            return step, (at_ref[which] if picked else 0)

        return pl.BlockSpec((depth, wide), place)

    whole = pl.BlockSpec((height, width), lambda step, at_ref: (0, 0))
    return pl.pallas_call(
        lambda *refs: block_kernel(depth, *refs),
        grid_spec=pltpu.PrefetchScalarGridSpec(
            num_scalar_prefetch=1,
            grid=(steps,),
            in_specs=[
                spec(height, 0, left_at is not None),
                spec(width, 1, right_at is not None),
                *[whole] * len(adds),
            ],
            out_specs=whole,
        ),
        out_shape=jax.ShapeDtypeStruct((height, width), F32),
        compiler_params=pltpu.CompilerParams(vmem_limit_bytes=32 * 1024 * 1024),
        name="block_product",
    )(at, left, right, *adds)


def group_scan(a, b, backward):
    place = lax.broadcasted_iota(jnp.int32, a.shape, 0)
    for step in (1, 2, 4):
        shift = 8 - step if backward else step
        inside = place < 8 - step if backward else place >= step
        a_shift = jnp.where(inside, pltpu.roll(a, shift, 0), 1.0)
        b_shift = jnp.where(inside, pltpu.roll(b, shift, 0), 0.0)
        b = a * b_shift + b
        a = a * a_shift
    return a, b


def forth_kernel(a_ref, b_ref, x_ref, p_ref, before_ref, p_before_ref):
    rows, width = a_ref.shape
    first = lax.broadcasted_iota(jnp.int32, (8, width), 0) == 0

    def last(value):
        return jnp.broadcast_to(value[7:8, :], (8, width))

    def run(begin, count, long):
        def body(step, carry):
            carry_x, carry_p = carry
            here = pl.ds(pl.multiple_of(begin + step * 8, 8), 8)
            decay = a_ref[here, :]
            a, b = group_scan(decay, b_ref[here, :], False)
            x = b + a * carry_x
            x_ref[here, :] = x
            before = jnp.where(first, carry_x, pltpu.roll(x, 1, 0))
            before_ref[here, :] = jnp.where(decay == 0.0, 0.0, before)
            if long:
                product = a * carry_p
                p_ref[here, :] = product
                p_before_ref[here, :] = jnp.where(first, carry_p, pltpu.roll(product, 1, 0))
                carry_p = last(product)
            return last(x), carry_p

        start = (jnp.zeros((8, width), F32), jnp.ones((8, width), F32))
        lax.fori_loop(0, count, body, start, unroll=4)

    run(0, LCHUNK // 8, True)
    run(LCHUNK, (rows - LCHUNK) // 8, False)


def back_kernel(a_ref, b_ref, x_ref, p_ref):
    rows, width = a_ref.shape
    end = lax.broadcasted_iota(jnp.int32, (8, width), 0) == 7

    def top(value):
        return jnp.broadcast_to(value[0:1, :], (8, width))

    def run(begin, count, long):
        def body(step, carry):
            carry_x, carry_p, carry_a = carry
            here = pl.ds(pl.multiple_of(begin + (count - 1 - step) * 8, 8), 8)
            decay = a_ref[here, :]
            link = jnp.where(end, carry_a, pltpu.roll(decay, 7, 0))
            a, b = group_scan(link, b_ref[here, :], True)
            x = b + a * carry_x
            x_ref[here, :] = x
            if long:
                product = a * carry_p
                p_ref[here, :] = product
                carry_p = top(product)
            return top(x), carry_p, top(decay)

        one = jnp.ones((8, width), F32)
        lax.fori_loop(0, count, body, (jnp.zeros((8, width), F32), one, one), unroll=4)

    run(0, LCHUNK // 8, True)
    run(LCHUNK, (rows - LCHUNK) // 8, False)


def scan(a, b, backward):
    rows, width = a.shape
    block = 256
    spec = pl.BlockSpec((rows, block), lambda i: (0, i))
    long_spec = pl.BlockSpec((LCHUNK, block), lambda i: (0, i))
    shape = jax.ShapeDtypeStruct((rows, width), F32)
    long_shape = jax.ShapeDtypeStruct((LCHUNK, width), F32)
    times = 1 if backward else 2
    return pl.pallas_call(
        back_kernel if backward else forth_kernel,
        grid=(width // block,),
        in_specs=[spec, spec],
        out_specs=[spec, long_spec] * times,
        out_shape=[shape, long_shape] * times,
        compiler_params=pltpu.CompilerParams(vmem_limit_bytes=24 * 1024 * 1024),
        cost_estimate=pl.CostEstimate(
            flops=rows * width * 12, bytes_accessed=rows * width * 14, transcendentals=0
        ),
        name="scan_back" if backward else "scan_forth",
    )(a, b)


def carry_of(decay, local, backward, *before):
    count, mine = lax.axis_size("seq"), lax.axis_index("seq")
    ends = jnp.stack([decay, local])
    if count != 8:
        pieces = lax.all_gather(ends, "seq")
        order = jnp.arange(count)
        total = jnp.zeros_like(local)
        for step in range(count):
            i = count - 1 - step if backward else step
            use = (order[i] > mine) if backward else (order[i] < mine)
            total = jnp.where(use, pieces[i, 0] * total + pieces[i, 1], total)
        return total, total
    partner = lax.ppermute(ends, "seq", Y_PAIRS)
    first = (mine % 2 == 1) if backward else (mine % 2 == 0)
    early = jnp.where(first, ends, partner)
    late = jnp.where(first, partner, ends)
    pair = after(jnp.stack([early[0] * late[0], late[0] * early[1] + late[1]]), *before)
    total = jnp.zeros_like(local)
    got = []
    for hops in (3, 2, 1):
        if backward:
            pairs = [(i + 2 * hops, i) for i in range(8 - 2 * hops)]
        else:
            pairs = [(i, i + 2 * hops) for i in range(8 - 2 * hops)]
        got.append(lax.ppermute(pair, "seq", pairs))
    for piece in got:
        total = piece[0] * total + piece[1]
    return jnp.where(first, total, partner[0] * total + partner[1]), partner


def small_psum(value):
    value = value + lax.ppermute(value, "mp", CORE_PAIRS)
    return value + lax.ppermute(value, "mp", X_PAIRS)


def summed_half(send, keep):
    value = keep + lax.ppermute(send, "mp", CORE_PAIRS)
    return value + lax.ppermute(value, "mp", X_PAIRS), value


def per_device(
    tokens,
    attn_gain,
    w_input,
    w_forget,
    w_rgate,
    gnorm_gain,
    lower_bound,
    w_out,
    mlp_gain,
    w_gate,
    w_up,
    w_down,
    local_lengths,
    cotangent,
):
    rows, width = tokens.shape
    short_rows = rows - LCHUNK
    count, mine = lax.axis_size("seq"), lax.axis_index("seq")
    fast = count == 8
    core = lax.axis_index("mp") % 2
    side = mine % 2
    chunks = ((LCHUNK, short_rows), (0, LCHUNK))

    def half(value, own, chunk, *before):
        first, size = chunk
        which = later(core if own else 1 - core, *before)
        return lax.dynamic_slice_in_dim(value, first + which * (size // 2), size // 2, 0)

    def swap_core(value):
        return lax.ppermute(value, "mp", CORE_PAIRS)

    def swap_y(value):
        return lax.ppermute(value, "seq", Y_PAIRS)

    def canonical(parts):
        out = []
        for own, other in (parts[1], parts[0]):
            out.append(jnp.where(core == 0, own, other))
            out.append(jnp.where(core == 0, other, own))
        return jnp.concatenate(out, axis=0)

    lengths_row = local_lengths[0]
    offsets = jnp.cumsum(lengths_row) - lengths_row
    starts = jnp.any(
        jnp.arange(short_rows, dtype=jnp.int32)[:, None] == offsets[None, :], axis=1
    )[:, None]

    sizes = [size // 2 for _, size in chunks]
    cot_own = [(half(cotangent, True, c), half(cotangent, False, c)) for c in chunks]

    def near_rows(value, *ready):
        own = after(lax.ppermute(value, "seq", Z_PAIRS), *ready)
        return [own, swap_core(own)]

    def near_cot(index, *before):
        value = near_rows(
            after(cot_own[index][0].astype(F32), *before),
            *pick("cot_ready", (middle_own[0], middle_own[1])),
        )
        h = sizes[index]
        return placed(value, 2 * h, [(0, 0, h, 0), (1, 0, h, h)])

    if fast:
        near_cots = [None, None]

    stream = tokens.astype(F32)
    first_gain = attn_gain.astype(F32)
    first_scale = lax.rsqrt(jnp.mean(stream * stream, axis=1, keepdims=True) + norm_eps)
    normed_one_wide = stream * first_scale * first_gain
    normed_one = normed_one_wide.astype(BF16)
    pre_forget = dot(normed_one, w_forget)
    pre_input = dot(normed_one, w_input)
    pre_rgate = dot(normed_one, w_rgate)
    forget_sig = jax.nn.sigmoid(pre_forget)
    forget = lower_bound + (1.0 - lower_bound) * forget_sig
    input_act = jax.nn.silu(pre_input)
    drive = input_act * (1.0 - forget)
    is_start = jnp.concatenate([jnp.zeros((LCHUNK, 1), bool), starts], axis=0)
    decay = jnp.where(is_start, 0.0, forget)
    states_local, long_decay, before_local, before_decay = scan(decay, drive, False)

    def entered(local, product, carry):
        return jnp.concatenate(
            [local[:LCHUNK] + product * carry[None, :], local[LCHUNK:]], axis=0
        )

    state_gain = gnorm_gain.astype(F32)
    rgate_act = jax.nn.silu(pre_rgate)
    second_gain = mlp_gain.astype(F32)

    def row_scale(values):
        return lax.rsqrt(jnp.mean(values * values, axis=1, keepdims=True) + norm_eps)

    def glu(normed, d_hid):
        gate = dot(normed, w_gate)
        up = dot(normed, w_up)
        act = jax.nn.silu(gate)
        hidden = (act * up).astype(BF16)
        d_gate = (d_hid * up * silu_slope(gate)).astype(BF16)
        d_up = (d_hid * act).astype(BF16)
        return hidden, d_gate, d_up

    states_of, scale_of, gated_of, middle_own, middle_other = [], [], [], [], []
    for index, (first, size) in enumerate(chunks):
        local = states_local[first : first + size]
        if index == 1:
            carry_in, _ = carry_of(
                long_decay[-1], states_local[LCHUNK - 1], False, *pick("prefix", (short_sent,))
            )
            local = local + long_decay * carry_in[None, :]
        squares = small_psum(jnp.sum(local * local, axis=1))
        scale = lax.rsqrt(squares / width + norm_eps)[:, None]
        gated = local * scale * state_gain * rgate_act[first : first + size]
        gated16 = gated.astype(BF16)
        states_of.append(local)
        scale_of.append(scale)
        gated_of.append(gated)
        h = size // 2
        send = dot(lax.dynamic_slice_in_dim(gated16, (1 - core) * h, h, 0), w_out)
        keep = dot(lax.dynamic_slice_in_dim(gated16, core * h, h, 0), w_out)
        if index == 0:
            short_sent = send
        total, kept = summed_half(send, keep)
        own = half(tokens, True, (first, size)).astype(F32) + total
        middle_own.append(own)
        middle_other.append(swap_core(own))

    if fast:
        near_cots = [near_cot(i, *pick("cot", (carry_in, short_sent))) for i in (0, 1)]
    cot_rows = jnp.concatenate(
        [part for pair in cot_own for part in pair], axis=0
    )
    d_hidden = right_dot(cot_rows, w_down)
    states = jnp.concatenate([states_of[1], states_of[0]], axis=0)
    state_scale = jnp.concatenate([scale_of[1], scale_of[0]], axis=0)
    gated_wide = jnp.concatenate([gated_of[1], gated_of[0]], axis=0)
    gated = gated_wide.astype(BF16)
    normed_state = states * state_scale

    offset = 0
    main, d_mid_own, d_mid_other, hat_grad, feeds = [], [], [], [], []
    for index, (first, size) in enumerate(chunks):
        h = size // 2
        middle = jnp.concatenate([middle_own[index], middle_other[index]], axis=0)
        scale = row_scale(middle)
        hat = middle * scale
        normed = (hat * second_gain).astype(BF16)
        hidden, d_gate, d_up = glu(normed, d_hidden[offset : offset + size])
        offset += size
        main.append((normed, hidden, d_gate, d_up))
        send = right_dot(d_gate[h:], w_gate) + right_dot(d_up[h:], w_up)
        keep = right_dot(d_gate[:h], w_gate) + right_dot(d_up[:h], w_up)
        d_normed, glu_kept = summed_half(send, keep)
        hat, scale = hat[:h], scale[:h]
        hat_grad.append(jnp.sum(d_normed * hat, axis=0))
        e = d_normed * second_gain
        turn = scale * (e - hat * jnp.mean(e * hat, axis=1, keepdims=True))
        d_mid_own.append(cot_own[index][0].astype(F32) + turn)
        d_mid_other.append(cot_own[index][1].astype(F32) + swap_core(turn))

    normed_two, hidden, d_gate, d_up = (
        jnp.concatenate([main[0][i], main[1][i]], axis=0) for i in range(4)
    )

    if fast:
        sets = [(cot_rows, normed_two, hidden, d_gate, d_up)]
        for own, cot in zip(middle_own, near_cots):
            normed = normed_rows(near_rows(own), after(second_gain, *pick("glu", (glu_kept,))))
            sets.append((cot, normed, *glu(normed, right_dot(cot, w_down))))
        arrived = sets[-1][1]
        cots, normed, hiddens, gates, ups = (
            jnp.concatenate(parts, axis=0) for parts in zip(*sets)
        )
        block = width // 8
        plane = mine // 2
        planes = (plane, jnp.bitwise_xor(plane, 2))
        h = rows // 2

        def columns(value, start):
            return lax.dynamic_slice_in_dim(value, start * block, block, 1)

        def part_down(i, y):
            return left_dot(hiddens, columns(cots, 2 * planes[i] + y))


        def two(value, *before):
            y = later(1 - side, *before)
            return jnp.concatenate([columns(value, 2 * planes[i] + y) for i in (1, 0)], axis=1)

        down_sent = part_down(1, 1 - side)
        down_got = swap_y(down_sent)

    d_branch_wide = canonical(list(zip(d_mid_own, d_mid_other)))
    if fast:
        d_branch_wide = after(d_branch_wide, *pick("branch", (down_sent, down_got)))
    d_branch = d_branch_wide.astype(BF16)
    d_gated = right_dot(d_branch, w_out)
    grad_gnorm = jnp.sum(d_gated * normed_state * rgate_act, axis=0)
    d_rgate_wide = d_gated * normed_state * state_gain * silu_slope(pre_rgate)
    d_normed = d_gated * state_gain * rgate_act
    inner = small_psum(jnp.sum(d_normed * normed_state, axis=1))
    d_normed_last = d_mid_own[1]
    for index, (first, size) in enumerate(chunks):
        size = size // 2
        start = later(0, *pick("feed", (d_normed_last, inner)))
        feeds.append(
            [
                dot(lax.dynamic_slice_in_dim(main[index][1], start + i * size, size, 0), w_down)
                for i in (1, 0)
            ]
        )
    if fast:
        inner = after(inner, *pick("inner", (down_got,)))
    d_states = state_scale * (d_normed - normed_state * (inner / width)[:, None])
    back_local, back_decay = scan(decay, d_states, True)
    suffix_order = pick("suffix", (down_got,)) if fast else []
    carried_in, carry_sent = carry_of(
        forget[0] * back_decay[0], forget[0] * back_local[0], True, *suffix_order
    )
    dn1_order = ()
    if fast:

        def swap_far(value):
            return lax.ppermute(value, "seq", FAR_PAIRS)

        far_down = part_down(1, later(side, *pick("far_down", (carry_sent, carried_in)))) + down_got
        far_down_got = swap_far(far_down)
        dn1_order = pick("dn1", (far_down_got, far_down))
        carried_in = after(carried_in, *pick("carried", (far_down,)))
    carried = entered(back_local, back_decay, carried_in)
    states_prev = entered(before_local, before_decay, carry_in)
    d_forget = carried * (states_prev - input_act)
    d_input_wide = carried * (1.0 - forget) * silu_slope(pre_input)
    d_pforget_wide = d_forget * (1.0 - lower_bound) * forget_sig * (1.0 - forget_sig)
    grad_bound = jnp.sum(d_forget * (1.0 - forget_sig), axis=0)
    d_input = d_input_wide.astype(BF16)
    d_pforget = d_pforget_wide.astype(BF16)
    d_rgate = d_rgate_wide.astype(BF16)

    d_stream, first_grad = [], []
    for index, chunk in enumerate(chunks):
        both = []
        for own in (False, True):
            both.append(
                right_dot(half(d_input, own, chunk, *dn1_order), w_input)
                + right_dot(half(d_pforget, own, chunk), w_forget)
                + right_dot(half(d_rgate, own, chunk), w_rgate)
            )
        d_normed_one, _ = summed_half(*both)
        part = half(tokens, True, chunk).astype(F32)
        scale = row_scale(part)
        hat = part * scale
        first_grad.append(jnp.sum(d_normed_one * hat, axis=0))
        e = d_normed_one * first_gain
        turn = scale * (e - hat * jnp.mean(e * hat, axis=1, keepdims=True))
        d_stream.append((d_mid_own[index] + turn, d_mid_other[index] + swap_core(turn)))
    grad_tokens = canonical(d_stream).astype(BF16)

    mixed = []
    for own, other, feed in zip(middle_own, middle_other, feeds):
        value, _ = summed_half(*feed)
        mixed.append((own + value, other + swap_core(value)))
    mixed_out = canonical(mixed).astype(BF16)

    channels = grad_gnorm.shape[0]
    sends = []
    if not fast:

        def scattered(value, dim):
            return lax.psum_scatter(value, "seq", scatter_dimension=dim, tiled=True)

        grads = (
            scattered(left_dot(normed_one, d_input), 0),
            scattered(left_dot(normed_one, d_pforget), 0),
            scattered(left_dot(normed_one, d_rgate), 0),
            scattered(left_dot(gated, d_branch), 1),
            scattered(left_dot(normed_two, d_gate), 0),
            scattered(left_dot(normed_two, d_up), 0),
            scattered(left_dot(hidden, cot_rows), 1),
        )
    else:
        def near_columns(value, before, *ready):
            parts = [
                lax.dynamic_slice(
                    value,
                    (later(core * h, *before), 2 * jnp.bitwise_xor(q, 1) * block),
                    (h, 2 * block),
                )
                for q in planes
            ]
            low, high = [(0, 0, h, 0), (1, 0, h, h)], [(0, 0, h, h), (1, 0, h, 0)]
            return placed(near_rows(jnp.concatenate(parts, axis=1)), rows, low, high, later(core, *ready))

        def near_whole(value, *ready):
            near = lax.ppermute(value, "seq", Z_PAIRS)
            return placed([near], rows, [(0, 0, rows, 0)], flip=later(0, *ready))

        def pair_columns(value):
            return jnp.concatenate(
                [lax.dynamic_slice_in_dim(value, 2 * q * block, 2 * block, 1) for q in planes],
                axis=1,
            )

        joined_wide = jnp.concatenate([d_input_wide, d_pforget_wide, d_rgate_wide], axis=1)
        near_one = near_columns(
            normed_one_wide, pick("one", (arrived, carried_in)), *pick("one_ready", (joined_wide,))
        )
        near_gated = near_whole(
            after(gated_wide, *pick("gated", (arrived, carried_in))),
            *pick("gated_ready", (joined_wide,)),
        )

        def mm(kind, left, left_at, right, right_at):
            if FL[kind]:
                return block_product(left, left_at, right, right_at)
            left = left if left_at is None else columns(left, left_at)
            right = right if right_at is None else columns(right, right_at)
            return left_dot(left, right)

        def part_gate(i, y):
            return mm("kernel", normed, 2 * planes[i] + y, gates, None)

        def part_up(i, y):
            return mm("kernel", normed, 2 * planes[i] + y, ups, None)

        def part_out(i, y):
            return mm("kernel_rec", both_gated, None, both_branch, 2 * i + y)

        def part_joined(i, y):
            return mm("kernel_rec", both_one, 2 * i + y, joined, None)

        gate_sent = left_dot(two(normed, *pick("gate", (carry_sent,))), gates)
        up_sent = left_dot(two(normed, *pick("gate", (carry_sent,))), ups)
        gate_both, up_both = swap_y(gate_sent), swap_y(up_sent)
        own_gate, own_up = gate_both[block:], up_both[block:]
        far_gate = part_gate(1, later(side, *pick("far_gate", (carried_in, joined_wide)))) + gate_both[:block]
        far_up = part_up(1, later(side, *pick("far_up", (carried_in, joined_wide, far_gate)))) + up_both[:block]
        far_gate_got, far_up_got = swap_far(far_gate), swap_far(far_up)
        near_joined = near_whole(
            joined_wide, *pick("joined", (far_down_got, far_gate_got, far_up, far_down))
        )
        near_branch = near_columns(
            d_branch_wide, pick("near_branch", (joined_wide, far_up)), *pick("branch_ready", (near_joined,))
        )
        mine_joined = jnp.concatenate([d_input, d_pforget, d_rgate], axis=1)
        joined = jnp.concatenate([mine_joined, near_joined], axis=0)
        both_one = jnp.concatenate([pair_columns(normed_one), near_one], axis=0)
        both_branch = jnp.concatenate([pair_columns(d_branch), near_branch], axis=0)
        both_gated = jnp.concatenate([gated, near_gated], axis=0)

        joined_sent = part_joined(1, 1 - side)
        out_sent = part_out(1, later(1 - side, *pick("out", (joined_sent,))))
        far_joined = part_joined(1, later(side, *pick("far_joined", (far_up_got, far_gate_got)))) + swap_y(
            joined_sent
        )
        far_out = part_out(1, later(side, *pick("far_out", (far_joined,)))) + swap_y(out_sent)

        def finish(part, got, name, own=None):
            if own is None:
                sent = part(0, later(1 - side, *pick("own_" + name, (up_sent, joined_sent, far_joined))))
                ends.append(sent)
                own = swap_y(sent)
            kept = part(0, later(side, *pick("end_" + name, (joined_sent, far_joined, far_out))))
            return kept + own + got

        ends = [far_joined, far_out]
        grad_w_down = finish(part_down, far_down_got, "down")
        grad_w_gate = finish(part_gate, far_gate_got, "gate", own_gate)
        grad_w_up = finish(part_up, far_up_got, "up", own_up)
        grad_joined = finish(part_joined, swap_far(far_joined), "joined")
        grad_w_out = finish(part_out, swap_far(far_out), "out")
        sends = ends[: FL["sends"]]
        grads = (
            grad_joined[:, :channels],
            grad_joined[:, channels : 2 * channels],
            grad_joined[:, 2 * channels :],
            grad_w_out,
            grad_w_gate,
            grad_w_up,
            grad_w_down,
        )

    rowsum = jnp.stack([sum(first_grad), sum(hat_grad)])
    rowsum = rowsum + swap_core(rowsum)
    pieces = jnp.concatenate(
        [
            rowsum.reshape(2, count, width // count).transpose(1, 0, 2).reshape(count, -1),
            grad_gnorm.reshape(count, -1),
            grad_bound.reshape(count, -1),
        ],
        axis=1,
    )
    if not fast:
        vectors = lax.psum_scatter(pieces, "seq", scatter_dimension=0, tiled=True)[0]
    elif FL["direct"]:
        pieces = after(pieces, *sends)
        vectors = lax.dynamic_index_in_dim(pieces, mine, 0, keepdims=False)
        for step in range(1, 8):
            piece = lax.dynamic_index_in_dim(pieces, jnp.bitwise_xor(mine, step), 0, keepdims=False)
            vectors += lax.ppermute(piece, "seq", [(i, i ^ step) for i in range(8)])
    else:
        pieces = after(pieces, *sends)
        for step in FL["steps"]:
            pieces = pieces + lax.ppermute(pieces, "seq", [(i, i ^ step) for i in range(8)])
        vectors = lax.dynamic_index_in_dim(pieces, mine, 0, keepdims=False)
    part, small = width // count, channels // count
    grad_attn, grad_mlp = vectors[:part], vectors[part : 2 * part]
    grad_gnorm = vectors[2 * part : 2 * part + small][None, :]
    grad_bound = vectors[2 * part + small :][None, :]

    return (
        mixed_out,
        grad_tokens,
        grad_attn,
        grads[0],
        grads[1],
        grads[2],
        grad_gnorm,
        grad_bound,
        grads[3],
        grad_mlp,
        grads[4],
        grads[5],
        grads[6],
    )


def solution(mesh):
    in_specs = (
        P("seq", None),
        P(),
        P(None, "mp"),
        P(None, "mp"),
        P(None, "mp"),
        P("mp"),
        P("mp"),
        P("mp", None),
        P(),
        P(None, "mp"),
        P(None, "mp"),
        P("mp", None),
        P("seq", None),
        P("seq", None),
    )
    out_specs = (
        P("seq", None),
        P("seq", None),
        P("seq"),
        P("seq", "mp"),
        P("seq", "mp"),
        P("seq", "mp"),
        P("mp", "seq"),
        P("mp", "seq"),
        P("mp", "seq"),
        P("seq"),
        P("seq", "mp"),
        P("seq", "mp"),
        P("mp", "seq"),
    )
    return jax.shard_map(
        per_device, mesh=mesh, in_specs=in_specs, out_specs=out_specs, check_vma=False
    )
```

```python
import jax
import jax.numpy as jnp
from jax import lax
from jax.experimental import pallas as pl
from jax.experimental.pallas import tpu as pltpu
from jax.sharding import PartitionSpec as P

LCHUNK = 256
norm_eps = 1e-06
FL = {'cot': (0,), 'cot_ready': (1,), 'prefix': (0,), 'glu': (), 'branch': (1,), 'inner': (0,), 'feed': (0,), 'one': (), 'one_ready': (0,), 'gated': (), 'gated_ready': (0,), 'kernel': 0, 'kernel_rec': 0, 'gate': (0,), 'far_down': (0,), 'far_gate': (0,), 'far_up': (0,), 'joined': (0,), 'near_branch': (), 'branch_ready': (), 'out': (0,), 'far_joined': (1,), 'far_out': (), 'own_down': (1,), 'own_gate': (2,), 'own_up': (2,), 'own_joined': (), 'own_out': (2,), 'end_down': (1, 2), 'end_gate': (1,), 'end_up': (1, 2), 'end_joined': (), 'end_out': (1,), 'sends': 2, 'direct': 0, 'steps': (2, 1, 4), 'dn1': (), 'carried': (), 'suffix': ()}
F32 = jnp.float32
BF16 = jnp.bfloat16

CORE_PAIRS = [(i, i ^ 1) for i in range(4)]
X_PAIRS = [(i, i ^ 2) for i in range(4)]
Y_PAIRS = [(i, i ^ 1) for i in range(8)]
Z_PAIRS = [(i, i ^ 2) for i in range(8)]
FAR_PAIRS = [(i, i ^ 4) for i in range(8)]


def dot(left, right):
    return jnp.dot(left, right, preferred_element_type=F32)


def left_dot(left, right):
    return lax.dot_general(left, right, (((0,), (0,)), ((), ())), preferred_element_type=F32)


def right_dot(left, right):
    return lax.dot_general(left, right, (((1,), (1,)), ((), ())), preferred_element_type=F32)


def silu_slope(values):
    sig = jax.nn.sigmoid(values)
    return sig * (1.0 + values * (1.0 - sig))


def pick(name, options):
    return [options[i] for i in FL[name]]


def spark(*others):
    firsts = [
        lax.reshape(lax.slice(other, (0,) * other.ndim, (1,) * other.ndim), ()).astype(F32)
        for other in others
    ]
    return sum(firsts) * 0.0


def after(value, *others):
    return value + spark(*others) if others else value


def later(index, *others):
    return index + spark(*others).astype(jnp.int32) if others else index


def place_kernel(moves, flip_ref, *refs):
    out_ref = refs[-1]
    for flip, plan in enumerate(moves):

        @pl.when((flip_ref[0] != 0) == bool(flip))
        def _():
            for index, source, size, target in plan:
                out_ref[target : target + size, :] = refs[index][source : source + size, :].astype(
                    BF16
                )


def placed(values, rows, plan, other_plan=None, flip=0):
    width = values[0].shape[1]
    block = 256
    moves = (plan,) if other_plan is None else (plan, other_plan)
    return pl.pallas_call(
        lambda *refs: place_kernel(moves, *refs),
        grid=(width // block,),
        in_specs=[pl.BlockSpec(memory_space=pltpu.SMEM)]
        + [pl.BlockSpec((value.shape[0], block), lambda i: (0, i)) for value in values],
        out_specs=pl.BlockSpec((rows, block), lambda i: (0, i)),
        out_shape=jax.ShapeDtypeStruct((rows, width), BF16),
        compiler_params=pltpu.CompilerParams(vmem_limit_bytes=24 * 1024 * 1024),
        cost_estimate=pl.CostEstimate(
            flops=rows * width, bytes_accessed=rows * width * 6, transcendentals=0
        ),
        name="placed",
    )(jnp.full((1,), flip, jnp.int32), *values)


def norm_kernel(gain_ref, *refs):
    out_ref = refs[-1]
    target = 0
    for ref in refs[:-1]:
        values = ref[...]
        scale = lax.rsqrt(jnp.mean(values * values, axis=1, keepdims=True) + norm_eps)
        size = values.shape[0]
        out_ref[target : target + size, :] = (values * scale * gain_ref[...]).astype(BF16)
        target += size


def normed_rows(values, gain):
    width = gain.shape[0]
    rows = sum(value.shape[0] for value in values)
    return pl.pallas_call(
        norm_kernel,
        out_shape=jax.ShapeDtypeStruct((rows, width), BF16),
        compiler_params=pltpu.CompilerParams(vmem_limit_bytes=32 * 1024 * 1024),
        cost_estimate=pl.CostEstimate(
            flops=rows * width * 5, bytes_accessed=rows * width * 6, transcendentals=rows
        ),
        name="normed_rows",
    )(gain[None, :], *values)


def block_kernel(depth, at_ref, left_ref, right_ref, *refs):
    out_ref = refs[-1]
    step = pl.program_id(0)
    product = lax.dot_general(
        left_ref[...], right_ref[...], (((0,), (0,)), ((), ())), preferred_element_type=F32
    )

    @pl.when(step == 0)
    def _():
        total = product
        for ref in refs[:-1]:
            total += ref[...]
        out_ref[...] = total

    @pl.when(step > 0)
    def _():
        out_ref[...] += product


def block_product(left, left_at, right, right_at, *adds):
    block = 256
    rows = left.shape[0]
    steps = 3
    depth = rows // steps
    height = left.shape[1] if left_at is None else block
    width = right.shape[1] if right_at is None else block
    at = jnp.stack([jnp.int32(0) if p is None else p for p in (left_at, right_at)])

    def spec(wide, which, picked):
        def place(step, at_ref):
            return step, (at_ref[which] if picked else 0)

        return pl.BlockSpec((depth, wide), place)

    whole = pl.BlockSpec((height, width), lambda step, at_ref: (0, 0))
    return pl.pallas_call(
        lambda *refs: block_kernel(depth, *refs),
        grid_spec=pltpu.PrefetchScalarGridSpec(
            num_scalar_prefetch=1,
            grid=(steps,),
            in_specs=[
                spec(height, 0, left_at is not None),
                spec(width, 1, right_at is not None),
                *[whole] * len(adds),
            ],
            out_specs=whole,
        ),
        out_shape=jax.ShapeDtypeStruct((height, width), F32),
        compiler_params=pltpu.CompilerParams(vmem_limit_bytes=32 * 1024 * 1024),
        name="block_product",
    )(at, left, right, *adds)


def group_scan(a, b, backward):
    place = lax.broadcasted_iota(jnp.int32, a.shape, 0)
    for step in (1, 2, 4):
        shift = 8 - step if backward else step
        inside = place < 8 - step if backward else place >= step
        a_shift = jnp.where(inside, pltpu.roll(a, shift, 0), 1.0)
        b_shift = jnp.where(inside, pltpu.roll(b, shift, 0), 0.0)
        b = a * b_shift + b
        a = a * a_shift
    return a, b


def forth_kernel(a_ref, b_ref, x_ref, p_ref, before_ref, p_before_ref):
    rows, width = a_ref.shape
    first = lax.broadcasted_iota(jnp.int32, (8, width), 0) == 0

    def last(value):
        return jnp.broadcast_to(value[7:8, :], (8, width))

    def run(begin, count, long):
        def body(step, carry):
            carry_x, carry_p = carry
            here = pl.ds(pl.multiple_of(begin + step * 8, 8), 8)
            decay = a_ref[here, :]
            a, b = group_scan(decay, b_ref[here, :], False)
            x = b + a * carry_x
            x_ref[here, :] = x
            before = jnp.where(first, carry_x, pltpu.roll(x, 1, 0))
            before_ref[here, :] = jnp.where(decay == 0.0, 0.0, before)
            if long:
                product = a * carry_p
                p_ref[here, :] = product
                p_before_ref[here, :] = jnp.where(first, carry_p, pltpu.roll(product, 1, 0))
                carry_p = last(product)
            return last(x), carry_p

        start = (jnp.zeros((8, width), F32), jnp.ones((8, width), F32))
        lax.fori_loop(0, count, body, start, unroll=4)

    run(0, LCHUNK // 8, True)
    run(LCHUNK, (rows - LCHUNK) // 8, False)


def back_kernel(a_ref, b_ref, x_ref, p_ref):
    rows, width = a_ref.shape
    end = lax.broadcasted_iota(jnp.int32, (8, width), 0) == 7

    def top(value):
        return jnp.broadcast_to(value[0:1, :], (8, width))

    def run(begin, count, long):
        def body(step, carry):
            carry_x, carry_p, carry_a = carry
            here = pl.ds(pl.multiple_of(begin + (count - 1 - step) * 8, 8), 8)
            decay = a_ref[here, :]
            link = jnp.where(end, carry_a, pltpu.roll(decay, 7, 0))
            a, b = group_scan(link, b_ref[here, :], True)
            x = b + a * carry_x
            x_ref[here, :] = x
            if long:
                product = a * carry_p
                p_ref[here, :] = product
                carry_p = top(product)
            return top(x), carry_p, top(decay)

        one = jnp.ones((8, width), F32)
        lax.fori_loop(0, count, body, (jnp.zeros((8, width), F32), one, one), unroll=4)

    run(0, LCHUNK // 8, True)
    run(LCHUNK, (rows - LCHUNK) // 8, False)


def scan(a, b, backward):
    rows, width = a.shape
    block = 256
    spec = pl.BlockSpec((rows, block), lambda i: (0, i))
    long_spec = pl.BlockSpec((LCHUNK, block), lambda i: (0, i))
    shape = jax.ShapeDtypeStruct((rows, width), F32)
    long_shape = jax.ShapeDtypeStruct((LCHUNK, width), F32)
    times = 1 if backward else 2
    return pl.pallas_call(
        back_kernel if backward else forth_kernel,
        grid=(width // block,),
        in_specs=[spec, spec],
        out_specs=[spec, long_spec] * times,
        out_shape=[shape, long_shape] * times,
        compiler_params=pltpu.CompilerParams(vmem_limit_bytes=24 * 1024 * 1024),
        cost_estimate=pl.CostEstimate(
            flops=rows * width * 12, bytes_accessed=rows * width * 14, transcendentals=0
        ),
        name="scan_back" if backward else "scan_forth",
    )(a, b)


def carry_of(decay, local, backward, *before):
    count, mine = lax.axis_size("seq"), lax.axis_index("seq")
    ends = jnp.stack([decay, local])
    if count != 8:
        pieces = lax.all_gather(ends, "seq")
        order = jnp.arange(count)
        total = jnp.zeros_like(local)
        for step in range(count):
            i = count - 1 - step if backward else step
            use = (order[i] > mine) if backward else (order[i] < mine)
            total = jnp.where(use, pieces[i, 0] * total + pieces[i, 1], total)
        return total, total
    partner = lax.ppermute(ends, "seq", Y_PAIRS)
    first = (mine % 2 == 1) if backward else (mine % 2 == 0)
    early = jnp.where(first, ends, partner)
    late = jnp.where(first, partner, ends)
    pair = after(jnp.stack([early[0] * late[0], late[0] * early[1] + late[1]]), *before)
    total = jnp.zeros_like(local)
    got = []
    for hops in (3, 2, 1):
        if backward:
            pairs = [(i + 2 * hops, i) for i in range(8 - 2 * hops)]
        else:
            pairs = [(i, i + 2 * hops) for i in range(8 - 2 * hops)]
        got.append(lax.ppermute(pair, "seq", pairs))
    for piece in got:
        total = piece[0] * total + piece[1]
    return jnp.where(first, total, partner[0] * total + partner[1]), partner


def small_psum(value):
    value = value + lax.ppermute(value, "mp", CORE_PAIRS)
    return value + lax.ppermute(value, "mp", X_PAIRS)


def summed_half(send, keep):
    value = keep + lax.ppermute(send, "mp", CORE_PAIRS)
    return value + lax.ppermute(value, "mp", X_PAIRS), value


def per_device(
    tokens,
    attn_gain,
    w_input,
    w_forget,
    w_rgate,
    gnorm_gain,
    lower_bound,
    w_out,
    mlp_gain,
    w_gate,
    w_up,
    w_down,
    local_lengths,
    cotangent,
):
    rows, width = tokens.shape
    short_rows = rows - LCHUNK
    count, mine = lax.axis_size("seq"), lax.axis_index("seq")
    fast = count == 8
    core = lax.axis_index("mp") % 2
    side = mine % 2
    chunks = ((LCHUNK, short_rows), (0, LCHUNK))

    def half(value, own, chunk, *before):
        first, size = chunk
        which = later(core if own else 1 - core, *before)
        return lax.dynamic_slice_in_dim(value, first + which * (size // 2), size // 2, 0)

    def swap_core(value):
        return lax.ppermute(value, "mp", CORE_PAIRS)

    def swap_y(value):
        return lax.ppermute(value, "seq", Y_PAIRS)

    def canonical(parts):
        out = []
        for own, other in (parts[1], parts[0]):
            out.append(jnp.where(core == 0, own, other))
            out.append(jnp.where(core == 0, other, own))
        return jnp.concatenate(out, axis=0)

    lengths_row = local_lengths[0]
    offsets = jnp.cumsum(lengths_row) - lengths_row
    starts = jnp.any(
        jnp.arange(short_rows, dtype=jnp.int32)[:, None] == offsets[None, :], axis=1
    )[:, None]

    sizes = [size // 2 for _, size in chunks]
    cot_own = [(half(cotangent, True, c), half(cotangent, False, c)) for c in chunks]

    def near_rows(value, *ready):
        own = after(lax.ppermute(value, "seq", Z_PAIRS), *ready)
        return [own, swap_core(own)]

    def near_cot(index, *before):
        value = near_rows(
            after(cot_own[index][0].astype(F32), *before),
            *pick("cot_ready", (middle_own[0], middle_own[1])),
        )
        h = sizes[index]
        return placed(value, 2 * h, [(0, 0, h, 0), (1, 0, h, h)])

    if fast:
        near_cots = [None, None]

    stream = tokens.astype(F32)
    first_gain = attn_gain.astype(F32)
    first_scale = lax.rsqrt(jnp.mean(stream * stream, axis=1, keepdims=True) + norm_eps)
    normed_one_wide = stream * first_scale * first_gain
    normed_one = normed_one_wide.astype(BF16)
    pre_forget = dot(normed_one, w_forget)
    pre_input = dot(normed_one, w_input)
    pre_rgate = dot(normed_one, w_rgate)
    forget_sig = jax.nn.sigmoid(pre_forget)
    forget = lower_bound + (1.0 - lower_bound) * forget_sig
    input_act = jax.nn.silu(pre_input)
    drive = input_act * (1.0 - forget)
    is_start = jnp.concatenate([jnp.zeros((LCHUNK, 1), bool), starts], axis=0)
    decay = jnp.where(is_start, 0.0, forget)
    states_local, long_decay, before_local, before_decay = scan(decay, drive, False)

    def entered(local, product, carry):
        return jnp.concatenate(
            [local[:LCHUNK] + product * carry[None, :], local[LCHUNK:]], axis=0
        )

    state_gain = gnorm_gain.astype(F32)
    rgate_act = jax.nn.silu(pre_rgate)
    second_gain = mlp_gain.astype(F32)

    def row_scale(values):
        return lax.rsqrt(jnp.mean(values * values, axis=1, keepdims=True) + norm_eps)

    def glu(normed, d_hid):
        gate = dot(normed, w_gate)
        up = dot(normed, w_up)
        act = jax.nn.silu(gate)
        hidden = (act * up).astype(BF16)
        d_gate = (d_hid * up * silu_slope(gate)).astype(BF16)
        d_up = (d_hid * act).astype(BF16)
        return hidden, d_gate, d_up

    states_of, scale_of, gated_of, middle_own, middle_other = [], [], [], [], []
    for index, (first, size) in enumerate(chunks):
        local = states_local[first : first + size]
        if index == 1:
            carry_in, _ = carry_of(
                long_decay[-1], states_local[LCHUNK - 1], False, *pick("prefix", (short_sent,))
            )
            local = local + long_decay * carry_in[None, :]
        squares = small_psum(jnp.sum(local * local, axis=1))
        scale = lax.rsqrt(squares / width + norm_eps)[:, None]
        gated = local * scale * state_gain * rgate_act[first : first + size]
        gated16 = gated.astype(BF16)
        states_of.append(local)
        scale_of.append(scale)
        gated_of.append(gated)
        h = size // 2
        send = dot(lax.dynamic_slice_in_dim(gated16, (1 - core) * h, h, 0), w_out)
        keep = dot(lax.dynamic_slice_in_dim(gated16, core * h, h, 0), w_out)
        if index == 0:
            short_sent = send
        total, kept = summed_half(send, keep)
        own = half(tokens, True, (first, size)).astype(F32) + total
        middle_own.append(own)
        middle_other.append(swap_core(own))

    if fast:
        near_cots = [near_cot(i, *pick("cot", (carry_in, short_sent))) for i in (0, 1)]
    cot_rows = jnp.concatenate(
        [part for pair in cot_own for part in pair], axis=0
    )
    d_hidden = right_dot(cot_rows, w_down)
    states = jnp.concatenate([states_of[1], states_of[0]], axis=0)
    state_scale = jnp.concatenate([scale_of[1], scale_of[0]], axis=0)
    gated_wide = jnp.concatenate([gated_of[1], gated_of[0]], axis=0)
    gated = gated_wide.astype(BF16)
    normed_state = states * state_scale

    offset = 0
    main, d_mid_own, d_mid_other, hat_grad, feeds = [], [], [], [], []
    for index, (first, size) in enumerate(chunks):
        h = size // 2
        middle = jnp.concatenate([middle_own[index], middle_other[index]], axis=0)
        scale = row_scale(middle)
        hat = middle * scale
        normed = (hat * second_gain).astype(BF16)
        hidden, d_gate, d_up = glu(normed, d_hidden[offset : offset + size])
        offset += size
        main.append((normed, hidden, d_gate, d_up))
        send = right_dot(d_gate[h:], w_gate) + right_dot(d_up[h:], w_up)
        keep = right_dot(d_gate[:h], w_gate) + right_dot(d_up[:h], w_up)
        d_normed, glu_kept = summed_half(send, keep)
        hat, scale = hat[:h], scale[:h]
        hat_grad.append(jnp.sum(d_normed * hat, axis=0))
        e = d_normed * second_gain
        turn = scale * (e - hat * jnp.mean(e * hat, axis=1, keepdims=True))
        d_mid_own.append(cot_own[index][0].astype(F32) + turn)
        d_mid_other.append(cot_own[index][1].astype(F32) + swap_core(turn))

    normed_two, hidden, d_gate, d_up = (
        jnp.concatenate([main[0][i], main[1][i]], axis=0) for i in range(4)
    )

    if fast:
        sets = [(cot_rows, normed_two, hidden, d_gate, d_up)]
        for own, cot in zip(middle_own, near_cots):
            normed = normed_rows(near_rows(own), after(second_gain, *pick("glu", (glu_kept,))))
            sets.append((cot, normed, *glu(normed, right_dot(cot, w_down))))
        arrived = sets[-1][1]
        cots, normed, hiddens, gates, ups = (
            jnp.concatenate(parts, axis=0) for parts in zip(*sets)
        )
        block = width // 8
        plane = mine // 2
        planes = (plane, jnp.bitwise_xor(plane, 2))
        h = rows // 2

        def columns(value, start):
            return lax.dynamic_slice_in_dim(value, start * block, block, 1)

        def part_down(i, y):
            return left_dot(hiddens, columns(cots, 2 * planes[i] + y))


        def two(value, *before):
            y = later(1 - side, *before)
            return jnp.concatenate([columns(value, 2 * planes[i] + y) for i in (1, 0)], axis=1)

        down_sent = part_down(1, 1 - side)
        down_got = swap_y(down_sent)

    d_branch_wide = canonical(list(zip(d_mid_own, d_mid_other)))
    if fast:
        d_branch_wide = after(d_branch_wide, *pick("branch", (down_sent, down_got)))
    d_branch = d_branch_wide.astype(BF16)
    d_gated = right_dot(d_branch, w_out)
    grad_gnorm = jnp.sum(d_gated * normed_state * rgate_act, axis=0)
    d_rgate_wide = d_gated * normed_state * state_gain * silu_slope(pre_rgate)
    d_normed = d_gated * state_gain * rgate_act
    inner = small_psum(jnp.sum(d_normed * normed_state, axis=1))
    d_normed_last = d_mid_own[1]
    for index, (first, size) in enumerate(chunks):
        size = size // 2
        start = later(0, *pick("feed", (d_normed_last, inner)))
        feeds.append(
            [
                dot(lax.dynamic_slice_in_dim(main[index][1], start + i * size, size, 0), w_down)
                for i in (1, 0)
            ]
        )
    if fast:
        inner = after(inner, *pick("inner", (down_got,)))
    d_states = state_scale * (d_normed - normed_state * (inner / width)[:, None])
    back_local, back_decay = scan(decay, d_states, True)
    suffix_order = pick("suffix", (down_got,)) if fast else []
    carried_in, carry_sent = carry_of(
        forget[0] * back_decay[0], forget[0] * back_local[0], True, *suffix_order
    )
    dn1_order = ()
    if fast:

        def swap_far(value):
            return lax.ppermute(value, "seq", FAR_PAIRS)

        far_down = part_down(1, later(side, *pick("far_down", (carry_sent, carried_in)))) + down_got
        far_down_got = swap_far(far_down)
        dn1_order = pick("dn1", (far_down_got, far_down))
        carried_in = after(carried_in, *pick("carried", (far_down,)))
    carried = entered(back_local, back_decay, carried_in)
    states_prev = entered(before_local, before_decay, carry_in)
    d_forget = carried * (states_prev - input_act)
    d_input_wide = carried * (1.0 - forget) * silu_slope(pre_input)
    d_pforget_wide = d_forget * (1.0 - lower_bound) * forget_sig * (1.0 - forget_sig)
    grad_bound = jnp.sum(d_forget * (1.0 - forget_sig), axis=0)
    d_input = d_input_wide.astype(BF16)
    d_pforget = d_pforget_wide.astype(BF16)
    d_rgate = d_rgate_wide.astype(BF16)

    d_stream, first_grad = [], []
    for index, chunk in enumerate(chunks):
        both = []
        for own in (False, True):
            both.append(
                right_dot(half(d_input, own, chunk, *dn1_order), w_input)
                + right_dot(half(d_pforget, own, chunk), w_forget)
                + right_dot(half(d_rgate, own, chunk), w_rgate)
            )
        d_normed_one, _ = summed_half(*both)
        part = half(tokens, True, chunk).astype(F32)
        scale = row_scale(part)
        hat = part * scale
        first_grad.append(jnp.sum(d_normed_one * hat, axis=0))
        e = d_normed_one * first_gain
        turn = scale * (e - hat * jnp.mean(e * hat, axis=1, keepdims=True))
        d_stream.append((d_mid_own[index] + turn, d_mid_other[index] + swap_core(turn)))
    grad_tokens = canonical(d_stream).astype(BF16)

    mixed = []
    for own, other, feed in zip(middle_own, middle_other, feeds):
        value, _ = summed_half(*feed)
        mixed.append((own + value, other + swap_core(value)))
    mixed_out = canonical(mixed).astype(BF16)

    channels = grad_gnorm.shape[0]
    sends = []
    if not fast:

        def scattered(value, dim):
            return lax.psum_scatter(value, "seq", scatter_dimension=dim, tiled=True)

        grads = (
            scattered(left_dot(normed_one, d_input), 0),
            scattered(left_dot(normed_one, d_pforget), 0),
            scattered(left_dot(normed_one, d_rgate), 0),
            scattered(left_dot(gated, d_branch), 1),
            scattered(left_dot(normed_two, d_gate), 0),
            scattered(left_dot(normed_two, d_up), 0),
            scattered(left_dot(hidden, cot_rows), 1),
        )
    else:
        def near_columns(value, before, *ready):
            parts = [
                lax.dynamic_slice(
                    value,
                    (later(core * h, *before), 2 * jnp.bitwise_xor(q, 1) * block),
                    (h, 2 * block),
                )
                for q in planes
            ]
            low, high = [(0, 0, h, 0), (1, 0, h, h)], [(0, 0, h, h), (1, 0, h, 0)]
            return placed(near_rows(jnp.concatenate(parts, axis=1)), rows, low, high, later(core, *ready))

        def near_whole(value, *ready):
            near = lax.ppermute(value, "seq", Z_PAIRS)
            return placed([near], rows, [(0, 0, rows, 0)], flip=later(0, *ready))

        def pair_columns(value):
            return jnp.concatenate(
                [lax.dynamic_slice_in_dim(value, 2 * q * block, 2 * block, 1) for q in planes],
                axis=1,
            )

        joined_wide = jnp.concatenate([d_input_wide, d_pforget_wide, d_rgate_wide], axis=1)
        near_one = near_columns(
            normed_one_wide, pick("one", (arrived, carried_in)), *pick("one_ready", (joined_wide,))
        )
        near_gated = near_whole(
            after(gated_wide, *pick("gated", (arrived, carried_in))),
            *pick("gated_ready", (joined_wide,)),
        )

        def mm(kind, left, left_at, right, right_at):
            if FL[kind]:
                return block_product(left, left_at, right, right_at)
            left = left if left_at is None else columns(left, left_at)
            right = right if right_at is None else columns(right, right_at)
            return left_dot(left, right)

        def part_gate(i, y):
            return mm("kernel", normed, 2 * planes[i] + y, gates, None)

        def part_up(i, y):
            return mm("kernel", normed, 2 * planes[i] + y, ups, None)

        def part_out(i, y):
            return mm("kernel_rec", both_gated, None, both_branch, 2 * i + y)

        def part_joined(i, y):
            return mm("kernel_rec", both_one, 2 * i + y, joined, None)

        gate_sent = left_dot(two(normed, *pick("gate", (carry_sent,))), gates)
        up_sent = left_dot(two(normed, *pick("gate", (carry_sent,))), ups)
        gate_both, up_both = swap_y(gate_sent), swap_y(up_sent)
        own_gate, own_up = gate_both[block:], up_both[block:]
        far_gate = part_gate(1, later(side, *pick("far_gate", (carried_in, joined_wide)))) + gate_both[:block]
        far_up = part_up(1, later(side, *pick("far_up", (carried_in, joined_wide, far_gate)))) + up_both[:block]
        far_gate_got, far_up_got = swap_far(far_gate), swap_far(far_up)
        near_joined = near_whole(
            joined_wide, *pick("joined", (far_down_got, far_gate_got, far_up, far_down))
        )
        near_branch = near_columns(
            d_branch_wide, pick("near_branch", (joined_wide, far_up)), *pick("branch_ready", (near_joined,))
        )
        mine_joined = jnp.concatenate([d_input, d_pforget, d_rgate], axis=1)
        joined = jnp.concatenate([mine_joined, near_joined], axis=0)
        both_one = jnp.concatenate([pair_columns(normed_one), near_one], axis=0)
        both_branch = jnp.concatenate([pair_columns(d_branch), near_branch], axis=0)
        both_gated = jnp.concatenate([gated, near_gated], axis=0)

        joined_sent = part_joined(1, 1 - side)
        out_sent = part_out(1, later(1 - side, *pick("out", (joined_sent,))))
        far_joined = part_joined(1, later(side, *pick("far_joined", (far_up_got, far_gate_got)))) + swap_y(
            joined_sent
        )
        far_out = part_out(1, later(side, *pick("far_out", (far_joined,)))) + swap_y(out_sent)

        def finish(part, got, name, own=None):
            if own is None:
                sent = part(0, later(1 - side, *pick("own_" + name, (up_sent, joined_sent, far_joined))))
                ends.append(sent)
                own = swap_y(sent)
            kept = part(0, later(side, *pick("end_" + name, (joined_sent, far_joined, far_out))))
            return kept + own + got

        ends = [far_joined, far_out]
        grad_w_down = finish(part_down, far_down_got, "down")
        grad_w_gate = finish(part_gate, far_gate_got, "gate", own_gate)
        grad_w_up = finish(part_up, far_up_got, "up", own_up)
        grad_joined = finish(part_joined, swap_far(far_joined), "joined")
        grad_w_out = finish(part_out, swap_far(far_out), "out")
        sends = ends[: FL["sends"]]
        grads = (
            grad_joined[:, :channels],
            grad_joined[:, channels : 2 * channels],
            grad_joined[:, 2 * channels :],
            grad_w_out,
            grad_w_gate,
            grad_w_up,
            grad_w_down,
        )

    rowsum = jnp.stack([sum(first_grad), sum(hat_grad)])
    rowsum = rowsum + swap_core(rowsum)
    pieces = jnp.concatenate(
        [
            rowsum.reshape(2, count, width // count).transpose(1, 0, 2).reshape(count, -1),
            grad_gnorm.reshape(count, -1),
            grad_bound.reshape(count, -1),
        ],
        axis=1,
    )
    if not fast:
        vectors = lax.psum_scatter(pieces, "seq", scatter_dimension=0, tiled=True)[0]
    elif FL["direct"]:
        pieces = after(pieces, *sends)
        vectors = lax.dynamic_index_in_dim(pieces, mine, 0, keepdims=False)
        for step in range(1, 8):
            piece = lax.dynamic_index_in_dim(pieces, jnp.bitwise_xor(mine, step), 0, keepdims=False)
            vectors += lax.ppermute(piece, "seq", [(i, i ^ step) for i in range(8)])
    else:
        pieces = after(pieces, *sends)
        for step in FL["steps"]:
            pieces = pieces + lax.ppermute(pieces, "seq", [(i, i ^ step) for i in range(8)])
        vectors = lax.dynamic_index_in_dim(pieces, mine, 0, keepdims=False)
    part, small = width // count, channels // count
    grad_attn, grad_mlp = vectors[:part], vectors[part : 2 * part]
    grad_gnorm = vectors[2 * part : 2 * part + small][None, :]
    grad_bound = vectors[2 * part + small :][None, :]

    return (
        mixed_out,
        grad_tokens,
        grad_attn,
        grads[0],
        grads[1],
        grads[2],
        grad_gnorm,
        grad_bound,
        grads[3],
        grad_mlp,
        grads[4],
        grads[5],
        grads[6],
    )


def solution(mesh):
    in_specs = (
        P("seq", None),
        P(),
        P(None, "mp"),
        P(None, "mp"),
        P(None, "mp"),
        P("mp"),
        P("mp"),
        P("mp", None),
        P(),
        P(None, "mp"),
        P(None, "mp"),
        P("mp", None),
        P("seq", None),
        P("seq", None),
    )
    out_specs = (
        P("seq", None),
        P("seq", None),
        P("seq"),
        P("seq", "mp"),
        P("seq", "mp"),
        P("seq", "mp"),
        P("mp", "seq"),
        P("mp", "seq"),
        P("mp", "seq"),
        P("seq"),
        P("seq", "mp"),
        P("seq", "mp"),
        P("mp", "seq"),
    )
    return jax.shard_map(
        per_device, mesh=mesh, in_specs=in_specs, out_specs=out_specs, check_vma=False
    )
```

```python
import jax
import jax.numpy as jnp
from jax import lax
from jax.experimental import pallas as pl
from jax.experimental.pallas import tpu as pltpu
from jax.sharding import PartitionSpec as P

LCHUNK = 256
norm_eps = 1e-06
FL = {'cot': (1,), 'cot_ready': (1,), 'prefix': (0,), 'glu': (), 'branch': (1,), 'inner': (0,), 'feed': (0,), 'one': (), 'one_ready': (0,), 'gated': (), 'gated_ready': (0,), 'kernel': 0, 'kernel_rec': 0, 'gate': (0,), 'far_down': (0,), 'far_gate': (0,), 'far_up': (0,), 'joined': (0,), 'near_branch': (), 'branch_ready': (), 'out': (0,), 'far_joined': (1,), 'far_out': (), 'own_down': (1,), 'own_gate': (2,), 'own_up': (2,), 'own_joined': (), 'own_out': (2,), 'end_down': (1, 2), 'end_gate': (1,), 'end_up': (1, 2), 'end_joined': (), 'end_out': (1,), 'sends': 2, 'direct': 0, 'steps': (2, 1, 4), 'dn1': (), 'carried': (), 'suffix': ()}
F32 = jnp.float32
BF16 = jnp.bfloat16

CORE_PAIRS = [(i, i ^ 1) for i in range(4)]
X_PAIRS = [(i, i ^ 2) for i in range(4)]
Y_PAIRS = [(i, i ^ 1) for i in range(8)]
Z_PAIRS = [(i, i ^ 2) for i in range(8)]
FAR_PAIRS = [(i, i ^ 4) for i in range(8)]


def dot(left, right):
    return jnp.dot(left, right, preferred_element_type=F32)


def left_dot(left, right):
    return lax.dot_general(left, right, (((0,), (0,)), ((), ())), preferred_element_type=F32)


def right_dot(left, right):
    return lax.dot_general(left, right, (((1,), (1,)), ((), ())), preferred_element_type=F32)


def silu_slope(values):
    sig = jax.nn.sigmoid(values)
    return sig * (1.0 + values * (1.0 - sig))


def pick(name, options):
    return [options[i] for i in FL[name]]


def spark(*others):
    firsts = [
        lax.reshape(lax.slice(other, (0,) * other.ndim, (1,) * other.ndim), ()).astype(F32)
        for other in others
    ]
    return sum(firsts) * 0.0


def after(value, *others):
    return value + spark(*others) if others else value


def later(index, *others):
    return index + spark(*others).astype(jnp.int32) if others else index


def place_kernel(moves, flip_ref, *refs):
    out_ref = refs[-1]
    for flip, plan in enumerate(moves):

        @pl.when((flip_ref[0] != 0) == bool(flip))
        def _():
            for index, source, size, target in plan:
                out_ref[target : target + size, :] = refs[index][source : source + size, :].astype(
                    BF16
                )


def placed(values, rows, plan, other_plan=None, flip=0):
    width = values[0].shape[1]
    block = 256
    moves = (plan,) if other_plan is None else (plan, other_plan)
    return pl.pallas_call(
        lambda *refs: place_kernel(moves, *refs),
        grid=(width // block,),
        in_specs=[pl.BlockSpec(memory_space=pltpu.SMEM)]
        + [pl.BlockSpec((value.shape[0], block), lambda i: (0, i)) for value in values],
        out_specs=pl.BlockSpec((rows, block), lambda i: (0, i)),
        out_shape=jax.ShapeDtypeStruct((rows, width), BF16),
        compiler_params=pltpu.CompilerParams(vmem_limit_bytes=24 * 1024 * 1024),
        cost_estimate=pl.CostEstimate(
            flops=rows * width, bytes_accessed=rows * width * 6, transcendentals=0
        ),
        name="placed",
    )(jnp.full((1,), flip, jnp.int32), *values)


def norm_kernel(gain_ref, *refs):
    out_ref = refs[-1]
    target = 0
    for ref in refs[:-1]:
        values = ref[...]
        scale = lax.rsqrt(jnp.mean(values * values, axis=1, keepdims=True) + norm_eps)
        size = values.shape[0]
        out_ref[target : target + size, :] = (values * scale * gain_ref[...]).astype(BF16)
        target += size


def normed_rows(values, gain):
    width = gain.shape[0]
    rows = sum(value.shape[0] for value in values)
    return pl.pallas_call(
        norm_kernel,
        out_shape=jax.ShapeDtypeStruct((rows, width), BF16),
        compiler_params=pltpu.CompilerParams(vmem_limit_bytes=32 * 1024 * 1024),
        cost_estimate=pl.CostEstimate(
            flops=rows * width * 5, bytes_accessed=rows * width * 6, transcendentals=rows
        ),
        name="normed_rows",
    )(gain[None, :], *values)


def block_kernel(depth, at_ref, left_ref, right_ref, *refs):
    out_ref = refs[-1]
    step = pl.program_id(0)
    product = lax.dot_general(
        left_ref[...], right_ref[...], (((0,), (0,)), ((), ())), preferred_element_type=F32
    )

    @pl.when(step == 0)
    def _():
        total = product
        for ref in refs[:-1]:
            total += ref[...]
        out_ref[...] = total

    @pl.when(step > 0)
    def _():
        out_ref[...] += product


def block_product(left, left_at, right, right_at, *adds):
    block = 256
    rows = left.shape[0]
    steps = 3
    depth = rows // steps
    height = left.shape[1] if left_at is None else block
    width = right.shape[1] if right_at is None else block
    at = jnp.stack([jnp.int32(0) if p is None else p for p in (left_at, right_at)])

    def spec(wide, which, picked):
        def place(step, at_ref):
            return step, (at_ref[which] if picked else 0)

        return pl.BlockSpec((depth, wide), place)

    whole = pl.BlockSpec((height, width), lambda step, at_ref: (0, 0))
    return pl.pallas_call(
        lambda *refs: block_kernel(depth, *refs),
        grid_spec=pltpu.PrefetchScalarGridSpec(
            num_scalar_prefetch=1,
            grid=(steps,),
            in_specs=[
                spec(height, 0, left_at is not None),
                spec(width, 1, right_at is not None),
                *[whole] * len(adds),
            ],
            out_specs=whole,
        ),
        out_shape=jax.ShapeDtypeStruct((height, width), F32),
        compiler_params=pltpu.CompilerParams(vmem_limit_bytes=32 * 1024 * 1024),
        name="block_product",
    )(at, left, right, *adds)


def group_scan(a, b, backward):
    place = lax.broadcasted_iota(jnp.int32, a.shape, 0)
    for step in (1, 2, 4):
        shift = 8 - step if backward else step
        inside = place < 8 - step if backward else place >= step
        a_shift = jnp.where(inside, pltpu.roll(a, shift, 0), 1.0)
        b_shift = jnp.where(inside, pltpu.roll(b, shift, 0), 0.0)
        b = a * b_shift + b
        a = a * a_shift
    return a, b


def forth_kernel(a_ref, b_ref, x_ref, p_ref, before_ref, p_before_ref):
    rows, width = a_ref.shape
    first = lax.broadcasted_iota(jnp.int32, (8, width), 0) == 0

    def last(value):
        return jnp.broadcast_to(value[7:8, :], (8, width))

    def run(begin, count, long):
        def body(step, carry):
            carry_x, carry_p = carry
            here = pl.ds(pl.multiple_of(begin + step * 8, 8), 8)
            decay = a_ref[here, :]
            a, b = group_scan(decay, b_ref[here, :], False)
            x = b + a * carry_x
            x_ref[here, :] = x
            before = jnp.where(first, carry_x, pltpu.roll(x, 1, 0))
            before_ref[here, :] = jnp.where(decay == 0.0, 0.0, before)
            if long:
                product = a * carry_p
                p_ref[here, :] = product
                p_before_ref[here, :] = jnp.where(first, carry_p, pltpu.roll(product, 1, 0))
                carry_p = last(product)
            return last(x), carry_p

        start = (jnp.zeros((8, width), F32), jnp.ones((8, width), F32))
        lax.fori_loop(0, count, body, start, unroll=4)

    run(0, LCHUNK // 8, True)
    run(LCHUNK, (rows - LCHUNK) // 8, False)


def back_kernel(a_ref, b_ref, x_ref, p_ref):
    rows, width = a_ref.shape
    end = lax.broadcasted_iota(jnp.int32, (8, width), 0) == 7

    def top(value):
        return jnp.broadcast_to(value[0:1, :], (8, width))

    def run(begin, count, long):
        def body(step, carry):
            carry_x, carry_p, carry_a = carry
            here = pl.ds(pl.multiple_of(begin + (count - 1 - step) * 8, 8), 8)
            decay = a_ref[here, :]
            link = jnp.where(end, carry_a, pltpu.roll(decay, 7, 0))
            a, b = group_scan(link, b_ref[here, :], True)
            x = b + a * carry_x
            x_ref[here, :] = x
            if long:
                product = a * carry_p
                p_ref[here, :] = product
                carry_p = top(product)
            return top(x), carry_p, top(decay)

        one = jnp.ones((8, width), F32)
        lax.fori_loop(0, count, body, (jnp.zeros((8, width), F32), one, one), unroll=4)

    run(0, LCHUNK // 8, True)
    run(LCHUNK, (rows - LCHUNK) // 8, False)


def scan(a, b, backward):
    rows, width = a.shape
    block = 256
    spec = pl.BlockSpec((rows, block), lambda i: (0, i))
    long_spec = pl.BlockSpec((LCHUNK, block), lambda i: (0, i))
    shape = jax.ShapeDtypeStruct((rows, width), F32)
    long_shape = jax.ShapeDtypeStruct((LCHUNK, width), F32)
    times = 1 if backward else 2
    return pl.pallas_call(
        back_kernel if backward else forth_kernel,
        grid=(width // block,),
        in_specs=[spec, spec],
        out_specs=[spec, long_spec] * times,
        out_shape=[shape, long_shape] * times,
        compiler_params=pltpu.CompilerParams(vmem_limit_bytes=24 * 1024 * 1024),
        cost_estimate=pl.CostEstimate(
            flops=rows * width * 12, bytes_accessed=rows * width * 14, transcendentals=0
        ),
        name="scan_back" if backward else "scan_forth",
    )(a, b)


def carry_of(decay, local, backward, *before):
    count, mine = lax.axis_size("seq"), lax.axis_index("seq")
    ends = jnp.stack([decay, local])
    if count != 8:
        pieces = lax.all_gather(ends, "seq")
        order = jnp.arange(count)
        total = jnp.zeros_like(local)
        for step in range(count):
            i = count - 1 - step if backward else step
            use = (order[i] > mine) if backward else (order[i] < mine)
            total = jnp.where(use, pieces[i, 0] * total + pieces[i, 1], total)
        return total, total
    partner = lax.ppermute(ends, "seq", Y_PAIRS)
    first = (mine % 2 == 1) if backward else (mine % 2 == 0)
    early = jnp.where(first, ends, partner)
    late = jnp.where(first, partner, ends)
    pair = after(jnp.stack([early[0] * late[0], late[0] * early[1] + late[1]]), *before)
    total = jnp.zeros_like(local)
    got = []
    for hops in (3, 2, 1):
        if backward:
            pairs = [(i + 2 * hops, i) for i in range(8 - 2 * hops)]
        else:
            pairs = [(i, i + 2 * hops) for i in range(8 - 2 * hops)]
        got.append(lax.ppermute(pair, "seq", pairs))
    for piece in got:
        total = piece[0] * total + piece[1]
    return jnp.where(first, total, partner[0] * total + partner[1]), partner


def small_psum(value):
    value = value + lax.ppermute(value, "mp", CORE_PAIRS)
    return value + lax.ppermute(value, "mp", X_PAIRS)


def summed_half(send, keep):
    value = keep + lax.ppermute(send, "mp", CORE_PAIRS)
    return value + lax.ppermute(value, "mp", X_PAIRS), value


def per_device(
    tokens,
    attn_gain,
    w_input,
    w_forget,
    w_rgate,
    gnorm_gain,
    lower_bound,
    w_out,
    mlp_gain,
    w_gate,
    w_up,
    w_down,
    local_lengths,
    cotangent,
):
    rows, width = tokens.shape
    short_rows = rows - LCHUNK
    count, mine = lax.axis_size("seq"), lax.axis_index("seq")
    fast = count == 8
    core = lax.axis_index("mp") % 2
    side = mine % 2
    chunks = ((LCHUNK, short_rows), (0, LCHUNK))

    def half(value, own, chunk, *before):
        first, size = chunk
        which = later(core if own else 1 - core, *before)
        return lax.dynamic_slice_in_dim(value, first + which * (size // 2), size // 2, 0)

    def swap_core(value):
        return lax.ppermute(value, "mp", CORE_PAIRS)

    def swap_y(value):
        return lax.ppermute(value, "seq", Y_PAIRS)

    def canonical(parts):
        out = []
        for own, other in (parts[1], parts[0]):
            out.append(jnp.where(core == 0, own, other))
            out.append(jnp.where(core == 0, other, own))
        return jnp.concatenate(out, axis=0)

    lengths_row = local_lengths[0]
    offsets = jnp.cumsum(lengths_row) - lengths_row
    starts = jnp.any(
        jnp.arange(short_rows, dtype=jnp.int32)[:, None] == offsets[None, :], axis=1
    )[:, None]

    sizes = [size // 2 for _, size in chunks]
    cot_own = [(half(cotangent, True, c), half(cotangent, False, c)) for c in chunks]

    def near_rows(value, *ready):
        own = after(lax.ppermute(value, "seq", Z_PAIRS), *ready)
        return [own, swap_core(own)]

    def near_cot(index, *before):
        value = near_rows(
            after(cot_own[index][0].astype(F32), *before),
            *pick("cot_ready", (middle_own[0], middle_own[1])),
        )
        h = sizes[index]
        return placed(value, 2 * h, [(0, 0, h, 0), (1, 0, h, h)])

    if fast:
        near_cots = [None, None]

    stream = tokens.astype(F32)
    first_gain = attn_gain.astype(F32)
    first_scale = lax.rsqrt(jnp.mean(stream * stream, axis=1, keepdims=True) + norm_eps)
    normed_one_wide = stream * first_scale * first_gain
    normed_one = normed_one_wide.astype(BF16)
    pre_forget = dot(normed_one, w_forget)
    pre_input = dot(normed_one, w_input)
    pre_rgate = dot(normed_one, w_rgate)
    forget_sig = jax.nn.sigmoid(pre_forget)
    forget = lower_bound + (1.0 - lower_bound) * forget_sig
    input_act = jax.nn.silu(pre_input)
    drive = input_act * (1.0 - forget)
    is_start = jnp.concatenate([jnp.zeros((LCHUNK, 1), bool), starts], axis=0)
    decay = jnp.where(is_start, 0.0, forget)
    states_local, long_decay, before_local, before_decay = scan(decay, drive, False)

    def entered(local, product, carry):
        return jnp.concatenate(
            [local[:LCHUNK] + product * carry[None, :], local[LCHUNK:]], axis=0
        )

    state_gain = gnorm_gain.astype(F32)
    rgate_act = jax.nn.silu(pre_rgate)
    second_gain = mlp_gain.astype(F32)

    def row_scale(values):
        return lax.rsqrt(jnp.mean(values * values, axis=1, keepdims=True) + norm_eps)

    def glu(normed, d_hid):
        gate = dot(normed, w_gate)
        up = dot(normed, w_up)
        act = jax.nn.silu(gate)
        hidden = (act * up).astype(BF16)
        d_gate = (d_hid * up * silu_slope(gate)).astype(BF16)
        d_up = (d_hid * act).astype(BF16)
        return hidden, d_gate, d_up

    states_of, scale_of, gated_of, middle_own, middle_other = [], [], [], [], []
    for index, (first, size) in enumerate(chunks):
        local = states_local[first : first + size]
        if index == 1:
            carry_in, _ = carry_of(
                long_decay[-1], states_local[LCHUNK - 1], False, *pick("prefix", (short_sent,))
            )
            local = local + long_decay * carry_in[None, :]
        squares = small_psum(jnp.sum(local * local, axis=1))
        scale = lax.rsqrt(squares / width + norm_eps)[:, None]
        gated = local * scale * state_gain * rgate_act[first : first + size]
        gated16 = gated.astype(BF16)
        states_of.append(local)
        scale_of.append(scale)
        gated_of.append(gated)
        h = size // 2
        send = dot(lax.dynamic_slice_in_dim(gated16, (1 - core) * h, h, 0), w_out)
        keep = dot(lax.dynamic_slice_in_dim(gated16, core * h, h, 0), w_out)
        if index == 0:
            short_sent = send
        total, kept = summed_half(send, keep)
        own = half(tokens, True, (first, size)).astype(F32) + total
        middle_own.append(own)
        middle_other.append(swap_core(own))

    if fast:
        near_cots = [near_cot(i, *pick("cot", (carry_in, short_sent))) for i in (0, 1)]
    cot_rows = jnp.concatenate(
        [part for pair in cot_own for part in pair], axis=0
    )
    d_hidden = right_dot(cot_rows, w_down)
    states = jnp.concatenate([states_of[1], states_of[0]], axis=0)
    state_scale = jnp.concatenate([scale_of[1], scale_of[0]], axis=0)
    gated_wide = jnp.concatenate([gated_of[1], gated_of[0]], axis=0)
    gated = gated_wide.astype(BF16)
    normed_state = states * state_scale

    offset = 0
    main, d_mid_own, d_mid_other, hat_grad, feeds = [], [], [], [], []
    for index, (first, size) in enumerate(chunks):
        h = size // 2
        middle = jnp.concatenate([middle_own[index], middle_other[index]], axis=0)
        scale = row_scale(middle)
        hat = middle * scale
        normed = (hat * second_gain).astype(BF16)
        hidden, d_gate, d_up = glu(normed, d_hidden[offset : offset + size])
        offset += size
        main.append((normed, hidden, d_gate, d_up))
        send = right_dot(d_gate[h:], w_gate) + right_dot(d_up[h:], w_up)
        keep = right_dot(d_gate[:h], w_gate) + right_dot(d_up[:h], w_up)
        d_normed, glu_kept = summed_half(send, keep)
        hat, scale = hat[:h], scale[:h]
        hat_grad.append(jnp.sum(d_normed * hat, axis=0))
        e = d_normed * second_gain
        turn = scale * (e - hat * jnp.mean(e * hat, axis=1, keepdims=True))
        d_mid_own.append(cot_own[index][0].astype(F32) + turn)
        d_mid_other.append(cot_own[index][1].astype(F32) + swap_core(turn))

    normed_two, hidden, d_gate, d_up = (
        jnp.concatenate([main[0][i], main[1][i]], axis=0) for i in range(4)
    )

    if fast:
        sets = [(cot_rows, normed_two, hidden, d_gate, d_up)]
        for own, cot in zip(middle_own, near_cots):
            normed = normed_rows(near_rows(own), after(second_gain, *pick("glu", (glu_kept,))))
            sets.append((cot, normed, *glu(normed, right_dot(cot, w_down))))
        arrived = sets[-1][1]
        cots, normed, hiddens, gates, ups = (
            jnp.concatenate(parts, axis=0) for parts in zip(*sets)
        )
        block = width // 8
        plane = mine // 2
        planes = (plane, jnp.bitwise_xor(plane, 2))
        h = rows // 2

        def columns(value, start):
            return lax.dynamic_slice_in_dim(value, start * block, block, 1)

        def part_down(i, y):
            return left_dot(hiddens, columns(cots, 2 * planes[i] + y))


        def two(value, *before):
            y = later(1 - side, *before)
            return jnp.concatenate([columns(value, 2 * planes[i] + y) for i in (1, 0)], axis=1)

        down_sent = part_down(1, 1 - side)
        down_got = swap_y(down_sent)

    d_branch_wide = canonical(list(zip(d_mid_own, d_mid_other)))
    if fast:
        d_branch_wide = after(d_branch_wide, *pick("branch", (down_sent, down_got)))
    d_branch = d_branch_wide.astype(BF16)
    d_gated = right_dot(d_branch, w_out)
    grad_gnorm = jnp.sum(d_gated * normed_state * rgate_act, axis=0)
    d_rgate_wide = d_gated * normed_state * state_gain * silu_slope(pre_rgate)
    d_normed = d_gated * state_gain * rgate_act
    inner = small_psum(jnp.sum(d_normed * normed_state, axis=1))
    d_normed_last = d_mid_own[1]
    for index, (first, size) in enumerate(chunks):
        size = size // 2
        start = later(0, *pick("feed", (d_normed_last, inner)))
        feeds.append(
            [
                dot(lax.dynamic_slice_in_dim(main[index][1], start + i * size, size, 0), w_down)
                for i in (1, 0)
            ]
        )
    if fast:
        inner = after(inner, *pick("inner", (down_got,)))
    d_states = state_scale * (d_normed - normed_state * (inner / width)[:, None])
    back_local, back_decay = scan(decay, d_states, True)
    suffix_order = pick("suffix", (down_got,)) if fast else []
    carried_in, carry_sent = carry_of(
        forget[0] * back_decay[0], forget[0] * back_local[0], True, *suffix_order
    )
    dn1_order = ()
    if fast:

        def swap_far(value):
            return lax.ppermute(value, "seq", FAR_PAIRS)

        far_down = part_down(1, later(side, *pick("far_down", (carry_sent, carried_in)))) + down_got
        far_down_got = swap_far(far_down)
        dn1_order = pick("dn1", (far_down_got, far_down))
        carried_in = after(carried_in, *pick("carried", (far_down,)))
    carried = entered(back_local, back_decay, carried_in)
    states_prev = entered(before_local, before_decay, carry_in)
    d_forget = carried * (states_prev - input_act)
    d_input_wide = carried * (1.0 - forget) * silu_slope(pre_input)
    d_pforget_wide = d_forget * (1.0 - lower_bound) * forget_sig * (1.0 - forget_sig)
    grad_bound = jnp.sum(d_forget * (1.0 - forget_sig), axis=0)
    d_input = d_input_wide.astype(BF16)
    d_pforget = d_pforget_wide.astype(BF16)
    d_rgate = d_rgate_wide.astype(BF16)

    d_stream, first_grad = [], []
    for index, chunk in enumerate(chunks):
        both = []
        for own in (False, True):
            both.append(
                right_dot(half(d_input, own, chunk, *dn1_order), w_input)
                + right_dot(half(d_pforget, own, chunk), w_forget)
                + right_dot(half(d_rgate, own, chunk), w_rgate)
            )
        d_normed_one, _ = summed_half(*both)
        part = half(tokens, True, chunk).astype(F32)
        scale = row_scale(part)
        hat = part * scale
        first_grad.append(jnp.sum(d_normed_one * hat, axis=0))
        e = d_normed_one * first_gain
        turn = scale * (e - hat * jnp.mean(e * hat, axis=1, keepdims=True))
        d_stream.append((d_mid_own[index] + turn, d_mid_other[index] + swap_core(turn)))
    grad_tokens = canonical(d_stream).astype(BF16)

    mixed = []
    for own, other, feed in zip(middle_own, middle_other, feeds):
        value, _ = summed_half(*feed)
        mixed.append((own + value, other + swap_core(value)))
    mixed_out = canonical(mixed).astype(BF16)

    channels = grad_gnorm.shape[0]
    sends = []
    if not fast:

        def scattered(value, dim):
            return lax.psum_scatter(value, "seq", scatter_dimension=dim, tiled=True)

        grads = (
            scattered(left_dot(normed_one, d_input), 0),
            scattered(left_dot(normed_one, d_pforget), 0),
            scattered(left_dot(normed_one, d_rgate), 0),
            scattered(left_dot(gated, d_branch), 1),
            scattered(left_dot(normed_two, d_gate), 0),
            scattered(left_dot(normed_two, d_up), 0),
            scattered(left_dot(hidden, cot_rows), 1),
        )
    else:
        def near_columns(value, before, *ready):
            parts = [
                lax.dynamic_slice(
                    value,
                    (later(core * h, *before), 2 * jnp.bitwise_xor(q, 1) * block),
                    (h, 2 * block),
                )
                for q in planes
            ]
            low, high = [(0, 0, h, 0), (1, 0, h, h)], [(0, 0, h, h), (1, 0, h, 0)]
            return placed(near_rows(jnp.concatenate(parts, axis=1)), rows, low, high, later(core, *ready))

        def near_whole(value, *ready):
            near = lax.ppermute(value, "seq", Z_PAIRS)
            return placed([near], rows, [(0, 0, rows, 0)], flip=later(0, *ready))

        def pair_columns(value):
            return jnp.concatenate(
                [lax.dynamic_slice_in_dim(value, 2 * q * block, 2 * block, 1) for q in planes],
                axis=1,
            )

        joined_wide = jnp.concatenate([d_input_wide, d_pforget_wide, d_rgate_wide], axis=1)
        near_one = near_columns(
            normed_one_wide, pick("one", (arrived, carried_in)), *pick("one_ready", (joined_wide,))
        )
        near_gated = near_whole(
            after(gated_wide, *pick("gated", (arrived, carried_in))),
            *pick("gated_ready", (joined_wide,)),
        )

        def mm(kind, left, left_at, right, right_at):
            if FL[kind]:
                return block_product(left, left_at, right, right_at)
            left = left if left_at is None else columns(left, left_at)
            right = right if right_at is None else columns(right, right_at)
            return left_dot(left, right)

        def part_gate(i, y):
            return mm("kernel", normed, 2 * planes[i] + y, gates, None)

        def part_up(i, y):
            return mm("kernel", normed, 2 * planes[i] + y, ups, None)

        def part_out(i, y):
            return mm("kernel_rec", both_gated, None, both_branch, 2 * i + y)

        def part_joined(i, y):
            return mm("kernel_rec", both_one, 2 * i + y, joined, None)

        gate_sent = left_dot(two(normed, *pick("gate", (carry_sent,))), gates)
        up_sent = left_dot(two(normed, *pick("gate", (carry_sent,))), ups)
        gate_both, up_both = swap_y(gate_sent), swap_y(up_sent)
        own_gate, own_up = gate_both[block:], up_both[block:]
        far_gate = part_gate(1, later(side, *pick("far_gate", (carried_in, joined_wide)))) + gate_both[:block]
        far_up = part_up(1, later(side, *pick("far_up", (carried_in, joined_wide, far_gate)))) + up_both[:block]
        far_gate_got, far_up_got = swap_far(far_gate), swap_far(far_up)
        near_joined = near_whole(
            joined_wide, *pick("joined", (far_down_got, far_gate_got, far_up, far_down))
        )
        near_branch = near_columns(
            d_branch_wide, pick("near_branch", (joined_wide, far_up)), *pick("branch_ready", (near_joined,))
        )
        mine_joined = jnp.concatenate([d_input, d_pforget, d_rgate], axis=1)
        joined = jnp.concatenate([mine_joined, near_joined], axis=0)
        both_one = jnp.concatenate([pair_columns(normed_one), near_one], axis=0)
        both_branch = jnp.concatenate([pair_columns(d_branch), near_branch], axis=0)
        both_gated = jnp.concatenate([gated, near_gated], axis=0)

        joined_sent = part_joined(1, 1 - side)
        out_sent = part_out(1, later(1 - side, *pick("out", (joined_sent,))))
        far_joined = part_joined(1, later(side, *pick("far_joined", (far_up_got, far_gate_got)))) + swap_y(
            joined_sent
        )
        far_out = part_out(1, later(side, *pick("far_out", (far_joined,)))) + swap_y(out_sent)

        def finish(part, got, name, own=None):
            if own is None:
                sent = part(0, later(1 - side, *pick("own_" + name, (up_sent, joined_sent, far_joined))))
                ends.append(sent)
                own = swap_y(sent)
            kept = part(0, later(side, *pick("end_" + name, (joined_sent, far_joined, far_out))))
            return kept + own + got

        ends = [far_joined, far_out]
        grad_w_down = finish(part_down, far_down_got, "down")
        grad_w_gate = finish(part_gate, far_gate_got, "gate", own_gate)
        grad_w_up = finish(part_up, far_up_got, "up", own_up)
        grad_joined = finish(part_joined, swap_far(far_joined), "joined")
        grad_w_out = finish(part_out, swap_far(far_out), "out")
        sends = ends[: FL["sends"]]
        grads = (
            grad_joined[:, :channels],
            grad_joined[:, channels : 2 * channels],
            grad_joined[:, 2 * channels :],
            grad_w_out,
            grad_w_gate,
            grad_w_up,
            grad_w_down,
        )

    rowsum = jnp.stack([sum(first_grad), sum(hat_grad)])
    rowsum = rowsum + swap_core(rowsum)
    pieces = jnp.concatenate(
        [
            rowsum.reshape(2, count, width // count).transpose(1, 0, 2).reshape(count, -1),
            grad_gnorm.reshape(count, -1),
            grad_bound.reshape(count, -1),
        ],
        axis=1,
    )
    if not fast:
        vectors = lax.psum_scatter(pieces, "seq", scatter_dimension=0, tiled=True)[0]
    elif FL["direct"]:
        pieces = after(pieces, *sends)
        vectors = lax.dynamic_index_in_dim(pieces, mine, 0, keepdims=False)
        for step in range(1, 8):
            piece = lax.dynamic_index_in_dim(pieces, jnp.bitwise_xor(mine, step), 0, keepdims=False)
            vectors += lax.ppermute(piece, "seq", [(i, i ^ step) for i in range(8)])
    else:
        pieces = after(pieces, *sends)
        for step in FL["steps"]:
            pieces = pieces + lax.ppermute(pieces, "seq", [(i, i ^ step) for i in range(8)])
        vectors = lax.dynamic_index_in_dim(pieces, mine, 0, keepdims=False)
    part, small = width // count, channels // count
    grad_attn, grad_mlp = vectors[:part], vectors[part : 2 * part]
    grad_gnorm = vectors[2 * part : 2 * part + small][None, :]
    grad_bound = vectors[2 * part + small :][None, :]

    return (
        mixed_out,
        grad_tokens,
        grad_attn,
        grads[0],
        grads[1],
        grads[2],
        grad_gnorm,
        grad_bound,
        grads[3],
        grad_mlp,
        grads[4],
        grads[5],
        grads[6],
    )


def solution(mesh):
    in_specs = (
        P("seq", None),
        P(),
        P(None, "mp"),
        P(None, "mp"),
        P(None, "mp"),
        P("mp"),
        P("mp"),
        P("mp", None),
        P(),
        P(None, "mp"),
        P(None, "mp"),
        P("mp", None),
        P("seq", None),
        P("seq", None),
    )
    out_specs = (
        P("seq", None),
        P("seq", None),
        P("seq"),
        P("seq", "mp"),
        P("seq", "mp"),
        P("seq", "mp"),
        P("mp", "seq"),
        P("mp", "seq"),
        P("mp", "seq"),
        P("seq"),
        P("seq", "mp"),
        P("seq", "mp"),
        P("mp", "seq"),
    )
    return jax.shard_map(
        per_device, mesh=mesh, in_specs=in_specs, out_specs=out_specs, check_vma=False
    )
```
